256 devices in a mesh: srow: 16 (over x, y_hi, core), scol: 16 (over z, y_lo).
Axes of the slice: x: 4, y: 4 (y_hi: 2, y_lo: 2; y = y_hi * 2 + y_lo), z: 8, core: 2. Of those that a mesh axis runs over, the one named last changes fastest.
Arguments:
- patterns: float32 [64, 64, 128, 128], P('srow', 'scol'), may hold values from 0.01 to 800, as said below
- offsets: int32 [64, 64, 2], P('srow', 'scol'), may hold values from 0 to 71, as said below
- object_field: float32 [2, 1152, 1152], P(None, 'srow', 'scol'), may hold values from -5 to 5
- probe: float32 [2, 2, 128, 128], replicated, may hold values from -6 to 6
Outputs:
- new_object: float32 [2, 1152, 1152], P(None, 'srow', 'scol')
- new_probe: float32 [2, 2, 128, 128], replicated
The draws below stay inside these ranges and needn't reach their ends.
Inputs may be any that keep to these rules, and one draw needn't show every extreme that they name: `patterns`: patterns are positive. `offsets`: position (r, c) has its centre at tile row 16 * (r mod 4) plus 0 to 23, and tile column 16 * (c mod 4) plus 0 to 23.
All inputs are finite; a program needn't handle non-finite values.
Results may differ from the reference program's by a relative error of at most 0.0003.
Values sent between devices are 32-bit elements; how exact they have to be, the bound alone decides.
No kernel may reach another device: no remote copies, remote signals or barrier semaphores. Data moves between devices by JAX's collectives and lax.ppermute only.
A program may use at most 64 MiB of HBM per device.

```python
import math
import jax
import jax.numpy as jnp
from jax import lax

W = 128
MODES = 2
STEP = 16
PAD = 8
PR = 4
PC = 4
OBJ_R = 72
OBJ_C = 72
NPR = 64
NPC = 64
OBJ_ROWS = 1152
OBJ_COLS = 1152


def draw_patterns(key, part):
    subkeys = jax.random.split(key, 3)
    row_frac = (jnp.arange(NPR, dtype=jnp.float32) + 0.5) / NPR
    col_frac = (jnp.arange(NPC, dtype=jnp.float32) + 0.5) / NPC
    levels = 2.0 * 3.0 ** (0.75 * row_frac[:, None] + 0.25 * col_frac[None, :])
    levels = levels * jax.random.uniform(subkeys[0], (NPR, NPC), jnp.float32, 0.7, 1.4)
    tilt_noise = jnp.clip(0.1 * jax.random.normal(subkeys[1], (2, NPR, NPC), jnp.float32), -0.3, 0.3)
    row_bend = 3.6 * ((row_frac - 0.5) ** 2 - 1.0 / 12.0)
    col_bend = 3.6 * ((col_frac - 0.5) ** 2 - 1.0 / 12.0)
    tilt_row = 0.6 * (row_frac[:, None] - 0.5) + 0.3 * (col_frac[None, :] - 0.5) + row_bend[:, None] + tilt_noise[0]
    tilt_col = -0.3 * (row_frac[:, None] - 0.5) + 0.6 * (col_frac[None, :] - 0.5) + col_bend[None, :] + tilt_noise[1]
    counter = jnp.arange(W, dtype=jnp.int32)
    frequency = ((counter + W // 2) % W - W // 2).astype(jnp.float32) * (2.0 / W)
    ramps = jnp.exp(tilt_row[:, :, None, None] * frequency[None, None, :, None] + tilt_col[:, :, None, None] * frequency[None, None, None, :])
    texture = jax.random.uniform(subkeys[2], (NPR, NPC, W, W), jnp.float32, 0.3, 1.7)
    return levels[:, :, None, None] * ramps * texture


def draw_offsets(key, part):
    jitter = jax.random.randint(key, (NPR, NPC, 2), 0, STEP + PAD, dtype=jnp.int32)
    base_row = jnp.arange(NPR, dtype=jnp.int32) % PR * STEP
    base_col = jnp.arange(NPC, dtype=jnp.int32) % PC * STEP
    drawn = jnp.stack([base_row[:, None] + jitter[:, :, 0], base_col[None, :] + jitter[:, :, 1]], axis=-1)
    drawn = drawn.at[0, 0].set(jnp.zeros((2,), jnp.int32))
    return drawn.at[PR - 1, PC - 1].set(jnp.array([OBJ_R - 1, OBJ_C - 1], dtype=jnp.int32))


def shard_levels(rng, shape, shards, least, high):
    def one(position, shards_of):
        heights = jax.random.uniform(jax.random.fold_in(jax.random.fold_in(rng, 6), position), (shards_of,), jnp.float32, least / len(shards), high / len(shards))
        return jnp.repeat(jnp.exp(heights), shape[position] // shards_of).reshape((-1,) + (1,) * (len(shape) - position - 1))

    level = one(*shards[0])
    for cut in shards[1:]:
        level = level * one(*cut)
    return level


def normal_values(stream_key, dims, scale, most, cuts=(), kind=jnp.bfloat16):
    values = scale * jax.random.normal(stream_key, dims, jnp.float32)
    if cuts:
        values = values * shard_levels(stream_key, dims, cuts, -0.22, 0.18)
    return jnp.clip(values, -most, most).astype(kind)


def setup_inputs(seed: int = 0) -> dict:
    arg_keys = jax.random.split(jax.random.key(seed), 5)
    return {
        "patterns": draw_patterns(jax.random.fold_in(arg_keys[4], 71), 0),
        "offsets": draw_offsets(jax.random.fold_in(arg_keys[4], 71), 0),
        "object_field": normal_values(arg_keys[2], (2, OBJ_ROWS, OBJ_COLS), 0.7, 5.0, ((1, 16), (2, 16)), jnp.float32),
        "probe": normal_values(arg_keys[3], (MODES, 2, W, W), 1.0, 6.0, (), jnp.float32),
    }


obj_rate = 0.2
probe_rate = 0.5
amp_floor = 0.1

def signed_freq(length):
    counter = jnp.arange(length, dtype=jnp.int32)
    return ((counter + length // 2) % length - length // 2).astype(jnp.float32)

def solve_three(matrix, right_side):
    crossed = jnp.stack([jnp.cross(matrix[1], matrix[2]), jnp.cross(matrix[2], matrix[0]), jnp.cross(matrix[0], matrix[1])])
    determ = jnp.sum(matrix[0] * crossed[0])
    return jnp.dot(crossed.T, right_side, precision=lax.Precision.HIGHEST) / determ

def reference(patterns, offsets, object_field, probe):
    highest = lax.Precision.HIGHEST
    frequency = signed_freq(W)
    weights = lax.optimization_barrier(jnp.sum(patterns, axis=(2, 3)))
    com_row = jnp.einsum('abij,i->ab', patterns, frequency, precision=highest) / weights
    com_col = jnp.einsum('abij,j->ab', patterns, frequency, precision=highest) / weights
    row_pos = (jnp.arange(NPR, dtype=jnp.float32) + 0.5) / NPR - 0.5
    col_pos = (jnp.arange(NPC, dtype=jnp.float32) + 0.5) / NPC - 0.5
    basis_set = jnp.stack([jnp.ones((NPR, NPC), jnp.float32), jnp.broadcast_to(row_pos[:, None], (NPR, NPC)), jnp.broadcast_to(col_pos[None, :], (NPR, NPC))])
    centres = jnp.stack([com_row, com_col])
    normal = jnp.einsum('iab,jab,ab->ij', basis_set, basis_set, weights, precision=highest)
    moments = jnp.einsum('iab,kab,ab->ik', basis_set, centres, weights, precision=highest)
    coeffs = solve_three(normal, moments)
    descan = jnp.einsum('iab,ik->kab', basis_set, coeffs, precision=highest)

    def shift_row(row_items):
        pattern_row, shift_r, shift_c = row_items
        spectrum = jnp.fft.fft2(pattern_row)
        phases = 2.0 * math.pi / W * (shift_r[:, None, None] * frequency[None, :, None] + shift_c[:, None, None] * frequency[None, None, :])
        turned = spectrum * lax.complex(jnp.cos(phases), jnp.sin(phases))
        return jnp.sqrt(jnp.maximum(jnp.real(jnp.fft.ifft2(turned)), 0.0))
    targets = lax.map(shift_row, (patterns, descan[0], descan[1]))
    obj_complex = lax.complex(object_field[0], object_field[1])
    probe_modes = lax.complex(probe[:, 0], probe[:, 1])
    pixel_steps = jnp.arange(W, dtype=jnp.int32)
    tile_rows = jnp.arange(NPR, dtype=jnp.int32) // PR * OBJ_R
    tile_cols = jnp.arange(NPC, dtype=jnp.int32) // PC * OBJ_C

    def one_row(carried, row_items):
        grad_obj, grad_probe = carried
        target_row, offset_row, tile_row = row_items
        centre_row = tile_row + offset_row[:, 0]
        centre_col = tile_cols + offset_row[:, 1]
        rows_at = (centre_row[:, None] - W // 2 + pixel_steps[None, :]) % OBJ_ROWS
        cols_at = (centre_col[:, None] - W // 2 + pixel_steps[None, :]) % OBJ_COLS
        window = obj_complex[rows_at[:, :, None], cols_at[:, None, :]]
        exit_waves = probe_modes[None] * window[:, None]
        far_field = jnp.fft.fft2(exit_waves, norm='ortho')
        amplitude = jnp.sqrt(lax.optimization_barrier(jnp.sum(jnp.real(far_field) ** 2 + jnp.imag(far_field) ** 2, axis=1)))
        factor = 1.0 - target_row / jnp.maximum(amplitude, amp_floor)
        back_wave = jnp.fft.ifft2(far_field * factor[:, None], norm='ortho')
        grad_window = lax.optimization_barrier(jnp.sum(jnp.conj(probe_modes)[None] * back_wave, axis=1))
        grad_obj = grad_obj.at[rows_at[:, :, None], cols_at[:, None, :]].add(grad_window)
        grad_probe = grad_probe + lax.optimization_barrier(jnp.sum(jnp.conj(window)[:, None] * back_wave, axis=0))
        return ((grad_obj, grad_probe), None)
    carried, _ = lax.scan(one_row, (jnp.zeros_like(obj_complex), jnp.zeros_like(probe_modes)), (targets, offsets, tile_rows))
    grad_obj, grad_probe = carried
    probe_power = jnp.max(lax.optimization_barrier(jnp.sum(probe * probe, axis=(0, 1))))
    updated_obj = obj_complex - obj_rate * grad_obj / probe_power
    updated_probe = probe_modes - probe_rate * grad_probe / (NPR * NPC)
    new_object = jnp.stack([jnp.real(updated_obj), jnp.imag(updated_obj)])
    new_probe = jnp.stack([jnp.real(updated_probe), jnp.imag(updated_probe)], axis=1)
    return (new_object, new_probe)
```

```python
import math

import jax
import jax.numpy as jnp
import ml_dtypes
import numpy as np
from jax import lax
from jax.experimental import pallas as pl
from jax.experimental.pallas import tpu as pltpu
from jax.sharding import PartitionSpec as P

W = 128
HALF = W // 2
MODES = 2
PR = 4
PC = 4
POSITIONS = PR * PC
TILE = 72
EXT = TILE + W

obj_rate = 0.2
probe_rate = 0.5
amp_floor = 0.1
highest = lax.Precision.HIGHEST
f32 = jnp.float32
bf16 = jnp.bfloat16


def dft_tables():
    counter = np.arange(W)
    angles = 2.0 * np.pi / W * (counter[:, None] * counter[None, :] % W)
    cos, sin = np.cos(angles), np.sin(angles)
    pair = np.block([[cos, -sin], [sin, cos]])

    def parts(matrix, axis):
        high = matrix.astype(ml_dtypes.bfloat16)
        low = (matrix - high.astype(np.float64)).astype(ml_dtypes.bfloat16)
        return np.concatenate([high, high, low], axis=axis)

    right_fwd = parts(pair / 16, 0)
    left_fwd = parts(pair.T / 8, 1)
    right_inv = parts(pair.T / 16, 0)
    left_inv = parts(pair / 8, 1)
    return right_fwd, left_fwd, right_inv, left_inv


def shift_tables():
    counter = np.arange(W)
    freq = np.where(counter <= HALF, counter, counter - HALF)
    angles = 2.0 * np.pi / W * (freq[:, None] * counter[None, :] % W)
    weight = np.where((counter == 0) | (counter == HALF), 1.0, 2.0)[:, None] / W
    is_cos = (counter <= HALF)[:, None]
    cols = np.where(is_cos, np.cos(angles), np.sin(angles)) * weight
    rows = np.where(is_cos, np.cos(angles), -np.sin(angles)) * weight
    return np.stack([cols, rows]).astype(np.float32)


def split(values):
    high = values.astype(bf16)
    low = (values - high.astype(f32)).astype(bf16)
    return high, low


def right_by(values, table):
    high, low = split(values)
    return jnp.dot(jnp.concatenate([high, low, high], axis=1), table, preferred_element_type=f32)


def left_by(table, values):
    high, low = split(values)
    return jnp.dot(table, jnp.concatenate([high, low, high], axis=0), preferred_element_type=f32)


def swap_blocks(values):
    top = jnp.concatenate([values[:W, :W], values[W:, :W]], axis=1)
    bottom = jnp.concatenate([values[:W, W:], values[W:, W:]], axis=1)
    return jnp.concatenate([top, bottom], axis=0)


def lane_iota(shape):
    return lax.broadcasted_iota(jnp.int32, shape, len(shape) - 1)


def row_iota(shape):
    return lax.broadcasted_iota(jnp.int32, shape, len(shape) - 2)


def place_of(place_ref, row_dev, col_dev, shape):
    position = row_iota(shape)
    row = (place_ref[0] * PR + position // PC).astype(f32)
    col = (place_ref[1] * PC + position % PC).astype(f32)
    return (row + 0.5) / (PR * row_dev) - 0.5, (col + 0.5) / (PC * col_dev) - 0.5


def sums_kernel(row_dev, col_dev, place_ref, patterns_ref, out_ref, total_ref, tilt_ref):
    k = row_iota((W, W))
    freq = (((k + HALF) % W) - HALF).astype(f32)
    for p in range(POSITIONS):
        pattern = patterns_ref[p]
        total_ref[p : p + 1, :] = jnp.sum(pattern, axis=0, keepdims=True)
        tilt_ref[p : p + 1, :] = jnp.sum(pattern * freq, axis=0, keepdims=True)
    lane = lane_iota((POSITIONS, W))
    col_freq = (((lane + HALF) % W) - HALF).astype(f32)
    total = total_ref[...]
    weight = jnp.sum(total, axis=1, keepdims=True)
    tilt_row = jnp.sum(tilt_ref[...], axis=1, keepdims=True)
    tilt_col = jnp.sum(total * col_freq, axis=1, keepdims=True)
    row, col = place_of(place_ref, row_dev, col_dev, (POSITIONS, W))
    terms = [
        weight,
        weight * row,
        weight * col,
        weight * row * row,
        weight * row * col,
        weight * col * col,
        tilt_row,
        tilt_row * row,
        tilt_row * col,
        tilt_col,
        tilt_col * row,
        tilt_col * col,
    ]
    packed = jnp.zeros((POSITIONS, W), f32)
    for i, term in enumerate(terms):
        packed = jnp.where(lane == i, term, packed)
    summed = jnp.sum(packed, axis=0, keepdims=True)
    out_ref[...] = jnp.broadcast_to(summed, out_ref.shape)


def cut_window(ext_ref, part, row, col):
    lane = lane_iota((W, W))
    shift = lax.rem(W - col, W)
    near = pltpu.roll(ext_ref[part, pl.ds(row, W), :], shift, 1)
    far = pltpu.roll(ext_ref[2 + part, pl.ds(row, W), :], shift, 1)
    return jnp.where(lane < W - col, near, far)


def forward_kernel(offsets_ref, ext_ref, probe_ref, right_ref, left_ref, far_ref, win_ref):
    def one(p, carried):
        row = offsets_ref[2 * p]
        col = offsets_ref[2 * p + 1]
        win_re = cut_window(ext_ref, 0, row, col)
        win_im = cut_window(ext_ref, 1, row, col)
        win_ref[p, 0] = win_re
        win_ref[p, 1] = win_im
        waves = []
        for m in range(MODES):
            probe_re, probe_im = probe_ref[2 * m], probe_ref[2 * m + 1]
            waves.append(
                jnp.concatenate(
                    [probe_re * win_re - probe_im * win_im, probe_re * win_im + probe_im * win_re],
                    axis=1,
                )
            )
        half_done = right_by(jnp.concatenate(waves, axis=0), right_ref[...])
        far_ref[p] = left_by(left_ref[...], swap_blocks(half_done))
        return carried

    lax.fori_loop(0, POSITIONS, one, 0, unroll=2)


def descan_of(sums, row, col):
    lane = lane_iota(sums.shape)
    pick = [
        jnp.sum(jnp.where(lane == i, sums, 0.0), axis=1, keepdims=True) for i in range(12)
    ]
    weight = pick[0]
    mean_row, mean_col = pick[1] / weight, pick[2] / weight
    var_row = pick[3] - mean_row * pick[1]
    var_both = pick[4] - mean_row * pick[2]
    var_col = pick[5] - mean_col * pick[2]
    determ = var_row * var_col - var_both * var_both
    shifts = []
    for first in (6, 9):
        tilt, tilt_row, tilt_col = pick[first : first + 3]
        cov_row = tilt_row - mean_row * tilt
        cov_col = tilt_col - mean_col * tilt
        slope_row = (var_col * cov_row - var_both * cov_col) / determ
        slope_col = (var_row * cov_col - var_both * cov_row) / determ
        shifts.append(tilt / weight + slope_row * (row - mean_row) + slope_col * (col - mean_col))
    return shifts


def circulant(line):
    return pltpu.roll(jnp.broadcast_to(line, (W, W)), 0, 1, stride=1, stride_axis=0)


def backward_kernel(
    row_dev,
    col_dev,
    offsets_ref,
    place_ref,
    sums_ref,
    patterns_ref,
    far_ref,
    win_ref,
    probe_ref,
    shift_ref,
    right_ref,
    left_ref,
    object_grad_ref,
    probe_grad_ref,
    cols_ref,
    rows_ref,
    nyquist_ref,
):
    sums = jnp.sum(sums_ref[...], axis=0, keepdims=True)
    row, col = place_of(place_ref, row_dev, col_dev, (POSITIONS, W))
    shift_row, shift_col = descan_of(sums, row, col)
    lane = lane_iota((POSITIONS, W))
    freq = jnp.where(lane <= HALF, lane, lane - HALF).astype(f32)
    quarter = jnp.where(lane <= HALF, 0.0, 0.25)

    def wave(shift):
        turns = freq * shift * (1.0 / W) + quarter
        return jnp.cos(2.0 * math.pi * (turns - jnp.round(turns)))

    def half_sine(shift):
        turns = shift * 0.5
        return jnp.sin(2.0 * math.pi * (turns - jnp.round(turns)))

    cols_ref[...] = jnp.dot(wave(shift_col), shift_ref[0], precision=highest)
    rows_ref[...] = jnp.dot(wave(shift_row), shift_ref[1], precision=highest)
    nyquist_ref[...] = half_sine(shift_row) * half_sine(shift_col) * (1.0 / (W * W))
    object_grad_ref[...] = jnp.zeros(object_grad_ref.shape, f32)
    probe_grad_ref[...] = jnp.zeros(probe_grad_ref.shape, f32)

    def one(p, carried):
        pattern = patterns_ref[p]
        place = row_iota((W, W)) + lane_iota((W, W))
        sign = (1 - 2 * (place & 1)).astype(f32)
        along_cols = circulant(cols_ref[pl.ds(p, 1), :])
        along_rows = circulant(rows_ref[pl.ds(p, 1), :])
        moved = jnp.dot(pattern, along_cols, precision=highest)
        moved = jnp.dot(along_rows, moved, precision=highest)
        alternate = jnp.sum(jnp.sum(pattern * sign, axis=0, keepdims=True), axis=1, keepdims=True)
        moved = moved - sign * (alternate * nyquist_ref[pl.ds(p, 1), :])
        target = jnp.sqrt(jnp.maximum(moved, 0.0))
        far = far_ref[p]
        power = far[:W, :W] ** 2 + far[:W, W:] ** 2 + far[W:, :W] ** 2 + far[W:, W:] ** 2
        factor = 1.0 - target / jnp.maximum(jnp.sqrt(power), amp_floor)
        wide = jnp.concatenate([factor, factor], axis=1)
        scaled = far * jnp.concatenate([wide, wide], axis=0)
        half_done = left_by(left_ref[...], scaled)
        back = right_by(swap_blocks(half_done), right_ref[...])
        win_re, win_im = win_ref[p, 0], win_ref[p, 1]
        grad_re = jnp.zeros((W, W), f32)
        grad_im = jnp.zeros((W, W), f32)
        for m in range(MODES):
            back_re, back_im = back[m * W : (m + 1) * W, :W], back[m * W : (m + 1) * W, W:]
            probe_re, probe_im = probe_ref[2 * m], probe_ref[2 * m + 1]
            grad_re += probe_re * back_re + probe_im * back_im
            grad_im += probe_re * back_im - probe_im * back_re
            probe_grad_ref[2 * m] += win_re * back_re + win_im * back_im
            probe_grad_ref[2 * m + 1] += win_re * back_im - win_im * back_re
        top = offsets_ref[2 * p]
        left = offsets_ref[2 * p + 1]
        lanes = lane_iota((W, W))
        for part, grad in enumerate((grad_re, grad_im)):
            turned = pltpu.roll(grad, left, 1)
            object_grad_ref[part, pl.ds(top, W), :] += jnp.where(lanes >= left, turned, 0.0)
            object_grad_ref[2 + part, pl.ds(top, W), :] += jnp.where(lanes < left, turned, 0.0)
        return carried

    lax.fori_loop(0, POSITIONS, one, 0)
    probe_power = (
        probe_ref[0] ** 2 + probe_ref[1] ** 2 + probe_ref[2] ** 2 + probe_ref[3] ** 2
    )
    peak = jnp.max(jnp.max(probe_power, axis=0, keepdims=True), axis=1, keepdims=True)
    object_grad_ref[...] = object_grad_ref[...] * (obj_rate / peak)[None]


def shifted_to(axis, step):
    count = lax.axis_size(axis)
    return [(i, (i + step) % count) for i in range(count)]


def spread(values, axis):
    return lax.all_to_all(values, axis, 0, 0, tiled=True)


SMEM = pl.BlockSpec(memory_space=pltpu.SMEM)
VMEM = pl.BlockSpec(memory_space=pltpu.VMEM)


def params(mib):
    return pltpu.CompilerParams(vmem_limit_bytes=mib * 1024 * 1024)


def on_device(patterns, offsets, object_field, probe):
    row_dev = lax.axis_size("srow")
    col_dev = lax.axis_size("scol")
    place = jnp.stack([lax.axis_index("srow"), lax.axis_index("scol")]).astype(jnp.int32)
    patterns = patterns.reshape(POSITIONS, W, W)
    offsets = offsets.reshape(2 * POSITIONS)
    probe_flat = probe.reshape(2 * MODES, W, W)
    right_fwd, left_fwd, right_inv, left_inv = (jnp.asarray(t) for t in dft_tables())
    shifts = jnp.asarray(shift_tables())

    above = lax.ppermute(object_field[:, TILE - HALF :, :], "srow", shifted_to("srow", 1))
    below = lax.ppermute(object_field[:, :HALF, :], "srow", shifted_to("srow", -1))

    sums = pl.pallas_call(
        lambda *refs: sums_kernel(row_dev, col_dev, *refs),
        out_shape=jax.ShapeDtypeStruct((row_dev, W), f32),
        in_specs=[SMEM, VMEM],
        out_specs=VMEM,
        scratch_shapes=[pltpu.VMEM((POSITIONS, W), f32), pltpu.VMEM((POSITIONS, W), f32)],
        compiler_params=params(8),
        name="sums",
    )(place, patterns)
    sums = spread(sums, "srow")

    tall = jnp.concatenate([above, object_field, below], axis=1)
    left_rim = lax.ppermute(tall[:, :, TILE - HALF :], "scol", shifted_to("scol", 1))
    right_rim = lax.ppermute(tall[:, :, :HALF], "scol", shifted_to("scol", -1))

    sums = jnp.broadcast_to(jnp.sum(sums, axis=0, keepdims=True), (col_dev, W))
    sums = spread(sums, "scol")

    near = jnp.concatenate([left_rim, tall[:, :, :HALF]], axis=2)
    blank = jnp.zeros((2, EXT, 2 * W - EXT), f32)
    far = jnp.concatenate([tall[:, :, HALF:], right_rim, blank], axis=2)
    ext = jnp.concatenate([near, far], axis=0)

    far, windows = pl.pallas_call(
        forward_kernel,
        out_shape=(
            jax.ShapeDtypeStruct((POSITIONS, 2 * W, 2 * W), f32),
            jax.ShapeDtypeStruct((POSITIONS, 2, W, W), f32),
        ),
        in_specs=[SMEM, VMEM, VMEM, VMEM, VMEM],
        out_specs=(VMEM, VMEM),
        compiler_params=params(24),
        name="forward",
    )(offsets, ext, probe_flat, right_fwd, left_fwd)

    ext_grad, probe_grad = pl.pallas_call(
        lambda *refs: backward_kernel(row_dev, col_dev, *refs),
        out_shape=(
            jax.ShapeDtypeStruct((4, EXT, W), f32),
            jax.ShapeDtypeStruct((2 * MODES, W, W), f32),
        ),
        in_specs=[SMEM, SMEM] + [VMEM] * 8,
        out_specs=(VMEM, VMEM),
        scratch_shapes=[pltpu.VMEM((POSITIONS, W), f32)] * 3,
        compiler_params=params(24),
        name="backward",
    )(offsets, place, sums, patterns, far, windows, probe_flat, shifts, right_inv, left_inv)

    from_below = lax.ppermute(ext_grad[:, :HALF, :], "srow", shifted_to("srow", -1))
    from_above = lax.ppermute(ext_grad[:, HALF + TILE :, :], "srow", shifted_to("srow", 1))

    chunk = 2 * MODES * W // row_dev
    parts = spread(probe_grad.reshape(row_dev, chunk, W), "srow")

    grad = ext_grad[:, HALF : HALF + TILE, :]
    grad = grad + jnp.pad(from_below, ((0, 0), (TILE - HALF, 0), (0, 0)))
    grad = grad + jnp.pad(from_above, ((0, 0), (0, TILE - HALF), (0, 0)))
    from_right = lax.ppermute(grad[:2, :, :HALF], "scol", shifted_to("scol", -1))
    from_left = lax.ppermute(
        grad[2:, :, TILE - HALF : TILE], "scol", shifted_to("scol", 1)
    )

    part = jnp.sum(parts, axis=0)
    part = spread(jnp.broadcast_to(part[None], (col_dev, chunk, W)), "scol")
    part = jnp.sum(part, axis=0)
    total = spread(jnp.broadcast_to(part[None], (row_dev, chunk, W)), "srow")

    grad = jnp.concatenate([grad[:2, :, HALF:], grad[2:, :, : TILE - HALF]], axis=2)
    grad = grad + jnp.pad(from_right, ((0, 0), (0, 0), (TILE - HALF, 0)))
    grad = grad + jnp.pad(from_left, ((0, 0), (0, 0), (0, TILE - HALF)))
    new_object = object_field - grad

    positions_all = POSITIONS * row_dev * col_dev
    new_probe = probe - (probe_rate / positions_all) * total.reshape(probe.shape)
    return new_object, new_probe


def solution(mesh):
    placed = (P("srow", "scol", None, None), P("srow", "scol", None), P(None, "srow", "scol"), P())
    return jax.shard_map(
        on_device,
        mesh=mesh,
        in_specs=placed,
        out_specs=(P(None, "srow", "scol"), P()),
        check_vma=False,
    )
```

```python
import math

import jax
import jax.numpy as jnp
import ml_dtypes
import numpy as np
from jax import lax
from jax.experimental import pallas as pl
from jax.experimental.pallas import tpu as pltpu
from jax.sharding import PartitionSpec as P

W = 128
HALF = W // 2
MODES = 2
PR = 4
PC = 4
POSITIONS = PR * PC
TILE = 72
EXT = TILE + W
GROUP = 4
AHEAD = 8

obj_rate = 0.2
probe_rate = 0.5
amp_floor = 0.1
highest = lax.Precision.HIGHEST
f32 = jnp.float32
bf16 = jnp.bfloat16


def dft_tables():
    counter = np.arange(W)
    angles = 2.0 * np.pi / W * (counter[:, None] * counter[None, :] % W)
    parts = []
    for table in (np.cos(angles), np.sin(angles)):
        high = table.astype(ml_dtypes.bfloat16)
        parts += [high, (table - high.astype(np.float64)).astype(ml_dtypes.bfloat16)]
    return np.stack(parts)


def shift_tables():
    counter = np.arange(W)
    freq = np.where(counter <= HALF, counter, counter - HALF)
    angles = 2.0 * np.pi / W * (freq[:, None] * counter[None, :] % W)
    weight = np.where((counter == 0) | (counter == HALF), 1.0, 2.0)[:, None] / W
    is_cos = (counter <= HALF)[:, None]
    cols = np.where(is_cos, np.cos(angles), np.sin(angles)) * weight
    rows = np.where(is_cos, np.cos(angles), -np.sin(angles)) * weight
    return np.stack([cols, rows]).astype(np.float32)


def split(values):
    high = values.astype(bf16)
    low = (values - high.astype(f32)).astype(bf16)
    return high, low


def fill_tables(tables_ref, right_ref, left_ref, inverse):
    for part in range(3):
        cos = tables_ref[part // 2]
        sin = tables_ref[2 + part // 2]
        plus, minus = (sin, -sin) if inverse else (-sin, sin)
        base = part * 2 * W
        right_ref[base : base + W, 0:W] = cos
        right_ref[base : base + W, W:] = plus
        right_ref[base + W : base + 2 * W, 0:W] = minus
        right_ref[base + W : base + 2 * W, W:] = cos
        scale = jnp.asarray(1.0 / W, bf16)
        left_ref[0:W, base : base + W] = cos * scale
        left_ref[0:W, base + W : base + 2 * W] = minus * scale
        left_ref[W:, base : base + W] = plus * scale
        left_ref[W:, base + W : base + 2 * W] = cos * scale


def by_parts(left, right):
    high, low = split(left)
    other_high, other_low = split(right)
    return jnp.dot(
        jnp.concatenate([high, low, high], axis=1),
        jnp.concatenate([other_high, other_high, other_low], axis=0),
        preferred_element_type=f32,
    )


def right_by(values, table):
    high, low = split(values)
    return jnp.dot(jnp.concatenate([high, low, high], axis=1), table, preferred_element_type=f32)


def left_by(table, values):
    high, low = split(values)
    return jnp.dot(table, jnp.concatenate([high, low, high], axis=0), preferred_element_type=f32)


def swap_blocks(values):
    top = jnp.concatenate([values[:W, :W], values[W:, :W]], axis=1)
    bottom = jnp.concatenate([values[:W, W:], values[W:, W:]], axis=1)
    return jnp.concatenate([top, bottom], axis=0)


def lane_iota(shape):
    return lax.broadcasted_iota(jnp.int32, shape, len(shape) - 1)


def row_iota(shape):
    return lax.broadcasted_iota(jnp.int32, shape, len(shape) - 2)


def place_of(place_ref, row_dev, col_dev, shape):
    position = row_iota(shape)
    row = (place_ref[0] * PR + position // PC).astype(f32)
    col = (place_ref[1] * PC + position % PC).astype(f32)
    return (row + 0.5) / (PR * row_dev) - 0.5, (col + 0.5) / (PC * col_dev) - 0.5


def sums_kernel(row_dev, col_dev, place_ref, patterns_ref, out_ref, total_ref, tilt_ref):
    k = row_iota((W, W))
    freq = (((k + HALF) % W) - HALF).astype(f32)
    for p in range(POSITIONS):
        pattern = patterns_ref[p]
        total_ref[p : p + 1, :] = jnp.sum(pattern, axis=0, keepdims=True)
        tilt_ref[p : p + 1, :] = jnp.sum(pattern * freq, axis=0, keepdims=True)
    lane = lane_iota((POSITIONS, W))
    col_freq = (((lane + HALF) % W) - HALF).astype(f32)
    total = total_ref[...]
    weight = jnp.sum(total, axis=1, keepdims=True)
    tilt_row = jnp.sum(tilt_ref[...], axis=1, keepdims=True)
    tilt_col = jnp.sum(total * col_freq, axis=1, keepdims=True)
    row, col = place_of(place_ref, row_dev, col_dev, (POSITIONS, W))
    terms = [
        weight,
        weight * row,
        weight * col,
        weight * row * row,
        weight * row * col,
        weight * col * col,
        tilt_row,
        tilt_row * row,
        tilt_row * col,
        tilt_col,
        tilt_col * row,
        tilt_col * col,
    ]
    packed = jnp.zeros((POSITIONS, W), f32)
    for i, term in enumerate(terms):
        packed = jnp.where(lane == i, term, packed)
    summed = jnp.sum(packed, axis=0, keepdims=True)
    out_ref[...] = jnp.broadcast_to(summed, out_ref.shape)


def cut_window(ext_ref, part, row, col):
    lane = lane_iota((W, W))
    shift = lax.rem(W - col, W)
    near = pltpu.roll(ext_ref[part, pl.ds(row, W), :], shift, 1)
    far = pltpu.roll(ext_ref[2 + part, pl.ds(row, W), :], shift, 1)
    return jnp.where(lane < W - col, near, far)


def forward_kernel(
    offsets_ref, ext_ref, probe_ref, tables_ref, far_out,
    right_ref, left_ref, far_ref, far_sem,
):
    fill_tables(tables_ref, right_ref, left_ref, False)

    def some(group, carried):
        places = [group * GROUP + i for i in range(GROUP)]
        waves = []
        for p in places:
            row, col = offsets_ref[2 * p], offsets_ref[2 * p + 1]
            win_re = cut_window(ext_ref, 0, row, col)
            win_im = cut_window(ext_ref, 1, row, col)
            for m in range(MODES):
                probe_re, probe_im = probe_ref[2 * m], probe_ref[2 * m + 1]
                wave_re = probe_re * win_re - probe_im * win_im
                wave_im = probe_re * win_im + probe_im * win_re
                waves.append(jnp.concatenate([wave_re, wave_im], axis=1))
        half_done = right_by(jnp.concatenate(waves, axis=0), right_ref[...])
        for i, p in enumerate(places):
            mine = half_done[i * 2 * W : (i + 1) * 2 * W]
            far_ref[p] = left_by(left_ref[...], swap_blocks(mine))
        copy_of(group).start()
        return carried

    def copy_of(group):
        part = pl.ds(group * GROUP, GROUP)
        return pltpu.make_async_copy(far_ref.at[part], far_out.at[part], far_sem.at[group])

    lax.fori_loop(0, POSITIONS // GROUP, some, 0)
    for group in range(POSITIONS // GROUP):
        copy_of(group).wait()


def descan_of(sums, row, col):
    lane = lane_iota(sums.shape)
    pick = [
        jnp.sum(jnp.where(lane == i, sums, 0.0), axis=1, keepdims=True) for i in range(12)
    ]
    weight = pick[0]
    mean_row, mean_col = pick[1] / weight, pick[2] / weight
    var_row = pick[3] - mean_row * pick[1]
    var_both = pick[4] - mean_row * pick[2]
    var_col = pick[5] - mean_col * pick[2]
    determ = var_row * var_col - var_both * var_both
    shifts = []
    for first in (6, 9):
        tilt, tilt_row, tilt_col = pick[first : first + 3]
        cov_row = tilt_row - mean_row * tilt
        cov_col = tilt_col - mean_col * tilt
        slope_row = (var_col * cov_row - var_both * cov_col) / determ
        slope_col = (var_row * cov_col - var_both * cov_row) / determ
        shifts.append(tilt / weight + slope_row * (row - mean_row) + slope_col * (col - mean_col))
    return shifts


def seed_of(line):
    return pltpu.roll(jnp.broadcast_to(line, (8, W)), 0, 1, stride=1, stride_axis=0)


def circulant(seed):
    return jnp.concatenate(
        [seed if i == 0 else pltpu.roll(seed, 8 * i, 1) for i in range(W // 8)], axis=0
    )


def backward_kernel(
    row_dev, col_dev, offsets_ref, place_ref, sums_ref, patterns_ref, far_in, ext_ref, probe_ref,
    shift_ref, tables_ref, object_grad_ref, probe_grad_ref,
    cols_ref, rows_ref, nyquist_ref, right_ref, left_ref, target_ref, far_ref, far_sem,
):
    far_copies = [
        pltpu.make_async_copy(far_in.at[part], far_ref.at[part], far_sem.at[i])
        for i, part in enumerate(pl.ds(i * GROUP, GROUP) for i in range(POSITIONS // GROUP))
    ]
    for copy in far_copies:
        copy.start()

    sums = jnp.sum(sums_ref[...], axis=0, keepdims=True)
    row, col = place_of(place_ref, row_dev, col_dev, (POSITIONS, W))
    shift_row, shift_col = descan_of(sums, row, col)
    lane = lane_iota((POSITIONS, W))
    freq = jnp.where(lane <= HALF, lane, lane - HALF).astype(f32)
    quarter = jnp.where(lane <= HALF, 0.0, 0.25)

    def wave(shift):
        turns = freq * shift * (1.0 / W) + quarter
        return jnp.cos(2.0 * math.pi * (turns - jnp.round(turns)))

    def half_sine(shift):
        turns = shift * 0.5
        return jnp.sin(2.0 * math.pi * (turns - jnp.round(turns)))

    cols = jnp.dot(wave(shift_col), shift_ref[0], precision=highest)
    rows = jnp.dot(wave(shift_row), shift_ref[1], precision=highest)
    for p in range(POSITIONS):
        cols_ref[p] = seed_of(cols[p : p + 1])
        rows_ref[p] = seed_of(rows[p : p + 1])
    nyquist_ref[...] = half_sine(shift_row) * half_sine(shift_col) * (1.0 / (W * W))
    fill_tables(tables_ref, right_ref, left_ref, True)
    object_grad_ref[...] = jnp.zeros(object_grad_ref.shape, f32)
    probe_grad_ref[...] = jnp.zeros(probe_grad_ref.shape, f32)

    def make_targets(group, carried):
        place = row_iota((W, W)) + lane_iota((W, W))
        sign = (1 - 2 * (place & 1)).astype(f32)
        for p in [group * AHEAD + i for i in range(AHEAD)]:
            pattern = patterns_ref[p]
            moved = by_parts(pattern, circulant(cols_ref[p]))
            moved = by_parts(circulant(rows_ref[p]), moved)
            alternate = jnp.sum(pattern * sign, axis=0, keepdims=True)
            alternate = jnp.sum(alternate, axis=1, keepdims=True)
            moved = moved - sign * (alternate * nyquist_ref[pl.ds(p, 1), :])
            target_ref[p] = jnp.sqrt(jnp.maximum(moved, 0.0))
        return carried

    lax.fori_loop(0, POSITIONS // AHEAD, make_targets, 0)

    def some(group, carried):
        places = [group * GROUP + i for i in range(GROUP)]
        halves = []
        for p in places:
            far = far_ref[p]
            power = far[:W, :W] ** 2 + far[:W, W:] ** 2 + far[W:, :W] ** 2 + far[W:, W:] ** 2
            factor = 1.0 - target_ref[p] / jnp.maximum(jnp.sqrt(power), amp_floor)
            wide = jnp.concatenate([factor, factor], axis=1)
            scaled = far * jnp.concatenate([wide, wide], axis=0)
            halves.append(swap_blocks(left_by(left_ref[...], scaled)))
        back = right_by(jnp.concatenate(halves, axis=0), right_ref[...])
        lanes = lane_iota((W, W))
        windows = []
        for p in places:
            at = offsets_ref[2 * p], offsets_ref[2 * p + 1]
            windows.append((cut_window(ext_ref, 0, *at), cut_window(ext_ref, 1, *at)))
        for m in range(MODES):
            sum_re = jnp.zeros((W, W), f32)
            sum_im = jnp.zeros((W, W), f32)
            for i, p in enumerate(places):
                base = i * 2 * W + m * W
                back_re, back_im = back[base : base + W, :W], back[base : base + W, W:]
                win_re, win_im = windows[i]
                sum_re += win_re * back_re + win_im * back_im
                sum_im += win_re * back_im - win_im * back_re
            probe_grad_ref[2 * m] += sum_re
            probe_grad_ref[2 * m + 1] += sum_im
        for i, p in enumerate(places):
            grads = [jnp.zeros((W, W), f32)] * 2
            for m in range(MODES):
                base = i * 2 * W + m * W
                back_re, back_im = back[base : base + W, :W], back[base : base + W, W:]
                probe_re, probe_im = probe_ref[2 * m], probe_ref[2 * m + 1]
                grads[0] += probe_re * back_re + probe_im * back_im
                grads[1] += probe_re * back_im - probe_im * back_re
            top, left = offsets_ref[2 * p], offsets_ref[2 * p + 1]
            for part, grad in enumerate(grads):
                turned = pltpu.roll(grad, left, 1)
                inside = jnp.where(lanes >= left, turned, 0.0)
                object_grad_ref[part, pl.ds(top, W), :] += inside
                object_grad_ref[2 + part, pl.ds(top, W), :] += turned - inside
        return carried

    for copy in far_copies:
        copy.wait()
    lax.fori_loop(0, POSITIONS // GROUP, some, 0)
    probe_power = (
        probe_ref[0] ** 2 + probe_ref[1] ** 2 + probe_ref[2] ** 2 + probe_ref[3] ** 2
    )
    peak = jnp.max(jnp.max(probe_power, axis=0, keepdims=True), axis=1, keepdims=True)
    object_grad_ref[...] = object_grad_ref[...] * (obj_rate / peak)[None]


def shifted_to(axis, step):
    count = lax.axis_size(axis)
    return [(i, (i + step) % count) for i in range(count)]


def spread(values, axis):
    return lax.all_to_all(values, axis, 0, 0, tiled=True)


SMEM = pl.BlockSpec(memory_space=pltpu.SMEM)
VMEM = pl.BlockSpec(memory_space=pltpu.VMEM)
HBM = pl.BlockSpec(memory_space=pltpu.HBM)


def params(mib):
    return pltpu.CompilerParams(vmem_limit_bytes=mib * 1024 * 1024)


def on_device(patterns, offsets, object_field, probe):
    row_dev = lax.axis_size("srow")
    col_dev = lax.axis_size("scol")
    place = jnp.stack([lax.axis_index("srow"), lax.axis_index("scol")]).astype(jnp.int32)
    patterns = patterns.reshape(POSITIONS, W, W)
    offsets = offsets.reshape(2 * POSITIONS)
    probe_flat = probe.reshape(2 * MODES, W, W)
    tables = jnp.asarray(dft_tables())
    shifts = jnp.asarray(shift_tables())

    above = lax.ppermute(object_field[:, TILE - HALF :, :], "srow", shifted_to("srow", 1))
    below = lax.ppermute(object_field[:, :HALF, :], "srow", shifted_to("srow", -1))

    sums = pl.pallas_call(
        lambda *refs: sums_kernel(row_dev, col_dev, *refs),
        out_shape=jax.ShapeDtypeStruct((row_dev * col_dev, W), f32),
        in_specs=[SMEM, VMEM],
        out_specs=VMEM,
        scratch_shapes=[pltpu.VMEM((POSITIONS, W), f32), pltpu.VMEM((POSITIONS, W), f32)],
        compiler_params=params(8),
        name="sums",
    )(place, patterns)
    above, below, sums = lax.optimization_barrier((above, below, sums))
    sums = spread(sums, ("srow", "scol"))

    tall = jnp.concatenate([above, object_field, below], axis=1)
    left_rim = lax.ppermute(tall[:, :, TILE - HALF :], "scol", shifted_to("scol", 1))
    right_rim = lax.ppermute(tall[:, :, :HALF], "scol", shifted_to("scol", -1))

    near = jnp.concatenate([left_rim, tall[:, :, :HALF]], axis=2)
    blank = jnp.zeros((2, EXT, 2 * W - EXT), f32)
    far = jnp.concatenate([tall[:, :, HALF:], right_rim, blank], axis=2)
    ext = jnp.concatenate([near, far], axis=0)

    big = [pltpu.VMEM((6 * W, 2 * W), bf16), pltpu.VMEM((2 * W, 6 * W), bf16)]
    far = pl.pallas_call(
        forward_kernel,
        out_shape=jax.ShapeDtypeStruct((POSITIONS, 2 * W, 2 * W), f32),
        in_specs=[SMEM, VMEM, VMEM, VMEM],
        out_specs=HBM,
        scratch_shapes=big
        + [
            pltpu.VMEM((POSITIONS, 2 * W, 2 * W), f32),
            pltpu.SemaphoreType.DMA((POSITIONS // GROUP,)),
        ],
        compiler_params=params(58),
        cost_estimate=pl.CostEstimate(flops=6 << 30, bytes_accessed=7 << 20, transcendentals=0),
        name="forward",
    )(offsets, ext, probe_flat, tables)

    ext_grad, probe_grad = pl.pallas_call(
        lambda *refs: backward_kernel(row_dev, col_dev, *refs),
        out_shape=(
            jax.ShapeDtypeStruct((4, EXT, W), f32),
            jax.ShapeDtypeStruct((2 * MODES, W, W), f32),
        ),
        in_specs=[SMEM, SMEM, VMEM, VMEM, HBM, VMEM, VMEM, VMEM, VMEM],
        out_specs=(VMEM, VMEM),
        scratch_shapes=[
            pltpu.VMEM((POSITIONS, 8, W), f32),
            pltpu.VMEM((POSITIONS, 8, W), f32),
            pltpu.VMEM((POSITIONS, W), f32),
        ]
        + big
        + [
            pltpu.VMEM((POSITIONS, W, W), f32),
            pltpu.VMEM((POSITIONS, 2 * W, 2 * W), f32),
            pltpu.SemaphoreType.DMA((POSITIONS // GROUP,)),
        ],
        compiler_params=params(58),
        cost_estimate=pl.CostEstimate(flops=8 << 30, bytes_accessed=9 << 20, transcendentals=0),
        name="backward",
    )(offsets, place, sums, patterns, far, ext, probe_flat, shifts, tables)

    from_below = lax.ppermute(ext_grad[:, :HALF, :], "srow", shifted_to("srow", -1))
    from_above = lax.ppermute(ext_grad[:, HALF + TILE :, :], "srow", shifted_to("srow", 1))

    chunk = 2 * MODES * W // row_dev
    parts = spread(probe_grad.reshape(row_dev, chunk, W), "srow")

    grad = ext_grad[:, HALF : HALF + TILE, :]
    grad = grad + jnp.pad(from_below, ((0, 0), (TILE - HALF, 0), (0, 0)))
    grad = grad + jnp.pad(from_above, ((0, 0), (0, TILE - HALF), (0, 0)))
    from_right = lax.ppermute(grad[:2, :, :HALF], "scol", shifted_to("scol", -1))
    from_left = lax.ppermute(
        grad[2:, :, TILE - HALF : TILE], "scol", shifted_to("scol", 1)
    )

    part = jnp.sum(parts, axis=0)
    part = spread(jnp.broadcast_to(part[None], (col_dev, chunk, W)), "scol")
    part = jnp.sum(part, axis=0)
    total = spread(jnp.broadcast_to(part[None], (row_dev, chunk, W)), "srow")

    grad = jnp.concatenate([grad[:2, :, HALF:], grad[2:, :, : TILE - HALF]], axis=2)
    grad = grad + jnp.pad(from_right, ((0, 0), (0, 0), (TILE - HALF, 0)))
    grad = grad + jnp.pad(from_left, ((0, 0), (0, 0), (0, TILE - HALF)))
    new_object = object_field - grad

    positions_all = POSITIONS * row_dev * col_dev
    new_probe = probe - (probe_rate / positions_all) * total.reshape(probe.shape)
    return new_object, new_probe


def solution(mesh):
    placed = (P("srow", "scol", None, None), P("srow", "scol", None), P(None, "srow", "scol"), P())
    return jax.shard_map(
        on_device,
        mesh=mesh,
        in_specs=placed,
        out_specs=(P(None, "srow", "scol"), P()),
        check_vma=False,
    )
```

```python
import math

import jax
import jax.numpy as jnp
import ml_dtypes
import numpy as np
from jax import lax
from jax.experimental import pallas as pl
from jax.experimental.pallas import tpu as pltpu
from jax.sharding import PartitionSpec as P

W = 128
HALF = W // 2
MODES = 2
PR = 4
PC = 4
POSITIONS = PR * PC
TILE = 72
EXT = TILE + W
GROUP = 8
AHEAD = 8

obj_rate = 0.2
probe_rate = 0.5
amp_floor = 0.1
highest = lax.Precision.HIGHEST
f32 = jnp.float32
bf16 = jnp.bfloat16


def dft_tables():
    counter = np.arange(W)
    angles = 2.0 * np.pi / W * (counter[:, None] * counter[None, :] % W)
    parts = []
    for table in (np.cos(angles), np.sin(angles)):
        high = table.astype(ml_dtypes.bfloat16)
        parts += [high, (table - high.astype(np.float64)).astype(ml_dtypes.bfloat16)]
    return np.stack(parts)


def shift_tables():
    counter = np.arange(W)
    freq = np.where(counter <= HALF, counter, counter - HALF)
    angles = 2.0 * np.pi / W * (freq[:, None] * counter[None, :] % W)
    weight = np.where((counter == 0) | (counter == HALF), 1.0, 2.0)[:, None] / W
    is_cos = (counter <= HALF)[:, None]
    cols = np.where(is_cos, np.cos(angles), np.sin(angles)) * weight
    rows = np.where(is_cos, np.cos(angles), -np.sin(angles)) * weight
    return np.stack([cols, rows]).astype(np.float32)


def split(values):
    high = values.astype(bf16)
    low = (values - high.astype(f32)).astype(bf16)
    return high, low


def fill_tables(tables_ref, right_ref, left_ref, inverse):
    for part in range(3):
        cos = tables_ref[part // 2]
        sin = tables_ref[2 + part // 2]
        plus, minus = (sin, -sin) if inverse else (-sin, sin)
        base = part * 2 * W
        right_ref[base : base + W, 0:W] = cos
        right_ref[base : base + W, W:] = plus
        right_ref[base + W : base + 2 * W, 0:W] = minus
        right_ref[base + W : base + 2 * W, W:] = cos
        scale = jnp.asarray(1.0 / W, bf16)
        left_ref[0:W, base : base + W] = cos * scale
        left_ref[0:W, base + W : base + 2 * W] = minus * scale
        left_ref[W:, base : base + W] = plus * scale
        left_ref[W:, base + W : base + 2 * W] = cos * scale


def by_parts(left, right):
    high, low = split(left)
    other_high, other_low = split(right)
    return jnp.dot(
        jnp.concatenate([high, low, high], axis=1),
        jnp.concatenate([other_high, other_high, other_low], axis=0),
        preferred_element_type=f32,
    )


def right_by(values, table):
    high, low = split(values)
    return jnp.dot(jnp.concatenate([high, low, high], axis=1), table, preferred_element_type=f32)


def left_by(table, values):
    high, low = split(values)
    return jnp.dot(table, jnp.concatenate([high, low, high], axis=0), preferred_element_type=f32)


def swap_blocks(values):
    top = jnp.concatenate([values[:W, :W], values[W:, :W]], axis=1)
    bottom = jnp.concatenate([values[:W, W:], values[W:, W:]], axis=1)
    return jnp.concatenate([top, bottom], axis=0)


def lane_iota(shape):
    return lax.broadcasted_iota(jnp.int32, shape, len(shape) - 1)


def row_iota(shape):
    return lax.broadcasted_iota(jnp.int32, shape, len(shape) - 2)


def place_of(scalars_ref, row_dev, col_dev, shape):
    position = row_iota(shape)
    row = (scalars_ref[2 * POSITIONS] * PR + position // PC).astype(f32)
    col = (scalars_ref[2 * POSITIONS + 1] * PC + position % PC).astype(f32)
    return (row + 0.5) / (PR * row_dev) - 0.5, (col + 0.5) / (PC * col_dev) - 0.5


def sums_kernel(row_dev, col_dev, scalars_ref, patterns_ref, out_ref, total_ref, tilt_ref):
    k = row_iota((W, W))
    freq = (((k + HALF) % W) - HALF).astype(f32)
    for p in range(POSITIONS):
        pattern = patterns_ref[p]
        total_ref[p : p + 1, :] = jnp.sum(pattern, axis=0, keepdims=True)
        tilt_ref[p : p + 1, :] = jnp.sum(pattern * freq, axis=0, keepdims=True)
    lane = lane_iota((POSITIONS, W))
    col_freq = (((lane + HALF) % W) - HALF).astype(f32)
    total = total_ref[...]
    weight = jnp.sum(total, axis=1, keepdims=True)
    tilt_row = jnp.sum(tilt_ref[...], axis=1, keepdims=True)
    tilt_col = jnp.sum(total * col_freq, axis=1, keepdims=True)
    row, col = place_of(scalars_ref, row_dev, col_dev, (POSITIONS, W))
    terms = [
        weight,
        weight * row,
        weight * col,
        weight * row * row,
        weight * row * col,
        weight * col * col,
        tilt_row,
        tilt_row * row,
        tilt_row * col,
        tilt_col,
        tilt_col * row,
        tilt_col * col,
    ]
    packed = jnp.zeros((POSITIONS, W), f32)
    for i, term in enumerate(terms):
        packed = jnp.where(lane == i, term, packed)
    summed = jnp.sum(packed, axis=0, keepdims=True)
    out_ref[...] = jnp.broadcast_to(summed, out_ref.shape)


def cut_window(ext_ref, part, row, col):
    lane = lane_iota((W, W))
    shift = lax.rem(W - col, W)
    near = pltpu.roll(ext_ref[part, pl.ds(row, W), :], shift, 1)
    far = pltpu.roll(ext_ref[2 + part, pl.ds(row, W), :], shift, 1)
    return jnp.where(lane < W - col, near, far)


def forward_kernel(
    scalars_ref, ext_ref, probe_ref, tables_ref, far_out,
    right_ref, left_ref, far_ref, far_sem,
):
    fill_tables(tables_ref, right_ref, left_ref, False)

    def some(group, carried):
        places = [group * GROUP + i for i in range(GROUP)]
        waves = []
        for p in places:
            row, col = scalars_ref[2 * p], scalars_ref[2 * p + 1]
            win_re = cut_window(ext_ref, 0, row, col)
            win_im = cut_window(ext_ref, 1, row, col)
            for m in range(MODES):
                probe_re, probe_im = probe_ref[2 * m], probe_ref[2 * m + 1]
                wave_re = probe_re * win_re - probe_im * win_im
                wave_im = probe_re * win_im + probe_im * win_re
                waves.append(jnp.concatenate([wave_re, wave_im], axis=1))
        half_done = right_by(jnp.concatenate(waves, axis=0), right_ref[...])
        for i, p in enumerate(places):
            mine = half_done[i * 2 * W : (i + 1) * 2 * W]
            far_ref[p] = left_by(left_ref[...], swap_blocks(mine))
        copy_of(group).start()
        return carried

    def copy_of(group):
        part = pl.ds(group * GROUP, GROUP)
        return pltpu.make_async_copy(far_ref.at[part], far_out.at[part], far_sem.at[group])

    lax.fori_loop(0, POSITIONS // GROUP, some, 0)
    for group in range(POSITIONS // GROUP):
        copy_of(group).wait()


def descan_of(sums, row, col):
    lane = lane_iota(sums.shape)
    pick = [
        jnp.sum(jnp.where(lane == i, sums, 0.0), axis=1, keepdims=True) for i in range(12)
    ]
    weight = pick[0]
    mean_row, mean_col = pick[1] / weight, pick[2] / weight
    var_row = pick[3] - mean_row * pick[1]
    var_both = pick[4] - mean_row * pick[2]
    var_col = pick[5] - mean_col * pick[2]
    determ = var_row * var_col - var_both * var_both
    shifts = []
    for first in (6, 9):
        tilt, tilt_row, tilt_col = pick[first : first + 3]
        cov_row = tilt_row - mean_row * tilt
        cov_col = tilt_col - mean_col * tilt
        slope_row = (var_col * cov_row - var_both * cov_col) / determ
        slope_col = (var_row * cov_col - var_both * cov_row) / determ
        shifts.append(tilt / weight + slope_row * (row - mean_row) + slope_col * (col - mean_col))
    return shifts


def seed_of(line):
    return pltpu.roll(jnp.broadcast_to(line, (8, W)), 0, 1, stride=1, stride_axis=0)


def circulant(seed):
    return jnp.concatenate(
        [seed if i == 0 else pltpu.roll(seed, 8 * i, 1) for i in range(W // 8)], axis=0
    )


def backward_kernel(
    row_dev, col_dev, scalars_ref, sums_ref, patterns_ref, far_in, ext_ref, probe_ref,
    shift_ref, tables_ref, object_grad_ref, probe_grad_ref,
    cols_ref, rows_ref, nyquist_ref, right_ref, left_ref, target_ref, far_ref, far_sem,
):
    far_copies = [
        pltpu.make_async_copy(far_in.at[part], far_ref.at[part], far_sem.at[i])
        for i, part in enumerate(pl.ds(i * GROUP, GROUP) for i in range(POSITIONS // GROUP))
    ]
    for copy in far_copies:
        copy.start()

    sums = jnp.sum(sums_ref[...], axis=0, keepdims=True)
    row, col = place_of(scalars_ref, row_dev, col_dev, (POSITIONS, W))
    shift_row, shift_col = descan_of(sums, row, col)
    lane = lane_iota((POSITIONS, W))
    freq = jnp.where(lane <= HALF, lane, lane - HALF).astype(f32)
    quarter = jnp.where(lane <= HALF, 0.0, 0.25)

    def wave(shift):
        turns = freq * shift * (1.0 / W) + quarter
        return jnp.cos(2.0 * math.pi * (turns - jnp.round(turns)))

    def half_sine(shift):
        turns = shift * 0.5
        return jnp.sin(2.0 * math.pi * (turns - jnp.round(turns)))

    cols = jnp.dot(wave(shift_col), shift_ref[0], precision=highest)
    rows = jnp.dot(wave(shift_row), shift_ref[1], precision=highest)
    for p in range(POSITIONS):
        cols_ref[p] = seed_of(cols[p : p + 1])
        rows_ref[p] = seed_of(rows[p : p + 1])
    nyquist_ref[...] = half_sine(shift_row) * half_sine(shift_col) * (1.0 / (W * W))
    fill_tables(tables_ref, right_ref, left_ref, True)
    object_grad_ref[...] = jnp.zeros(object_grad_ref.shape, f32)
    probe_grad_ref[...] = jnp.zeros(probe_grad_ref.shape, f32)

    def make_targets(group, carried):
        place = row_iota((W, W)) + lane_iota((W, W))
        sign = (1 - 2 * (place & 1)).astype(f32)
        for p in [group * AHEAD + i for i in range(AHEAD)]:
            pattern = patterns_ref[p]
            moved = by_parts(pattern, circulant(cols_ref[p]))
            moved = by_parts(circulant(rows_ref[p]), moved)
            alternate = jnp.sum(pattern * sign, axis=0, keepdims=True)
            alternate = jnp.sum(alternate, axis=1, keepdims=True)
            moved = moved - sign * (alternate * nyquist_ref[pl.ds(p, 1), :])
            target_ref[p] = jnp.sqrt(jnp.maximum(moved, 0.0))
        return carried

    lax.fori_loop(0, POSITIONS // AHEAD, make_targets, 0)

    def some(group, carried):
        places = [group * GROUP + i for i in range(GROUP)]
        halves = []
        for p in places:
            far = far_ref[p]
            power = far[:W, :W] ** 2 + far[:W, W:] ** 2 + far[W:, :W] ** 2 + far[W:, W:] ** 2
            factor = 1.0 - target_ref[p] / jnp.maximum(jnp.sqrt(power), amp_floor)
            wide = jnp.concatenate([factor, factor], axis=1)
            scaled = far * jnp.concatenate([wide, wide], axis=0)
            halves.append(swap_blocks(left_by(left_ref[...], scaled)))
        back = right_by(jnp.concatenate(halves, axis=0), right_ref[...])
        lanes = lane_iota((W, W))
        windows = []
        for p in places:
            at = scalars_ref[2 * p], scalars_ref[2 * p + 1]
            windows.append((cut_window(ext_ref, 0, *at), cut_window(ext_ref, 1, *at)))
        for m in range(MODES):
            sum_re = jnp.zeros((W, W), f32)
            sum_im = jnp.zeros((W, W), f32)
            for i, p in enumerate(places):
                base = i * 2 * W + m * W
                back_re, back_im = back[base : base + W, :W], back[base : base + W, W:]
                win_re, win_im = windows[i]
                sum_re += win_re * back_re + win_im * back_im
                sum_im += win_re * back_im - win_im * back_re
            probe_grad_ref[2 * m] += sum_re
            probe_grad_ref[2 * m + 1] += sum_im
        for i, p in enumerate(places):
            grads = [jnp.zeros((W, W), f32)] * 2
            for m in range(MODES):
                base = i * 2 * W + m * W
                back_re, back_im = back[base : base + W, :W], back[base : base + W, W:]
                probe_re, probe_im = probe_ref[2 * m], probe_ref[2 * m + 1]
                grads[0] += probe_re * back_re + probe_im * back_im
                grads[1] += probe_re * back_im - probe_im * back_re
            top, left = scalars_ref[2 * p], scalars_ref[2 * p + 1]
            for part, grad in enumerate(grads):
                turned = pltpu.roll(grad, left, 1)
                inside = jnp.where(lanes >= left, turned, 0.0)
                object_grad_ref[part, pl.ds(top, W), :] += inside
                object_grad_ref[2 + part, pl.ds(top, W), :] += turned - inside
        return carried

    for copy in far_copies:
        copy.wait()
    lax.fori_loop(0, POSITIONS // GROUP, some, 0)
    probe_power = (
        probe_ref[0] ** 2 + probe_ref[1] ** 2 + probe_ref[2] ** 2 + probe_ref[3] ** 2
    )
    peak = jnp.max(jnp.max(probe_power, axis=0, keepdims=True), axis=1, keepdims=True)
    object_grad_ref[...] = object_grad_ref[...] * (obj_rate / peak)[None]


def shifted_to(axis, step):
    count = lax.axis_size(axis)
    return [(i, (i + step) % count) for i in range(count)]


def spread(values, groups=None):
    return lax.all_to_all(
        values, ("srow", "scol"), 0, 0, axis_index_groups=groups, tiled=True
    )


def two_levels(row_dev, col_dev):
    near, across = [], []
    for pair in range(col_dev // 2):
        near.append([r * col_dev + 2 * pair + c for r in range(row_dev) for c in range(2)])
    for r in range(row_dev):
        for c in range(2):
            across.append([r * col_dev + 2 * pair + c for pair in range(col_dev // 2)])
    return near, across


SMEM = pl.BlockSpec(memory_space=pltpu.SMEM)
VMEM = pl.BlockSpec(memory_space=pltpu.VMEM)
HBM = pl.BlockSpec(memory_space=pltpu.HBM)


def params(mib):
    return pltpu.CompilerParams(vmem_limit_bytes=mib * 1024 * 1024)


def on_device(patterns, offsets, object_field, probe):
    row_dev = lax.axis_size("srow")
    col_dev = lax.axis_size("scol")
    place = jnp.stack([lax.axis_index("srow"), lax.axis_index("scol")]).astype(jnp.int32)
    scalars = jnp.concatenate([offsets.reshape(2 * POSITIONS), place])
    patterns = patterns.reshape(POSITIONS, W, W)
    probe_flat = probe.reshape(2 * MODES, W, W)
    tables = jnp.asarray(dft_tables())
    shifts = jnp.asarray(shift_tables())

    above = lax.ppermute(object_field[:, TILE - HALF :, :], "srow", shifted_to("srow", 1))
    below = lax.ppermute(object_field[:, :HALF, :], "srow", shifted_to("srow", -1))

    sums = pl.pallas_call(
        lambda *refs: sums_kernel(row_dev, col_dev, *refs),
        out_shape=jax.ShapeDtypeStruct((row_dev * col_dev, W), f32),
        in_specs=[SMEM, VMEM],
        out_specs=VMEM,
        scratch_shapes=[pltpu.VMEM((POSITIONS, W), f32), pltpu.VMEM((POSITIONS, W), f32)],
        compiler_params=params(8),
        name="sums",
    )(scalars, patterns)
    above, below, _ = lax.optimization_barrier((above, below, sums))
    sums = spread(sums.reshape(row_dev * col_dev, 1, W)).reshape(row_dev * col_dev, W)

    tall = jnp.concatenate([above, object_field, below], axis=1)
    left_rim = lax.ppermute(tall[:, :, TILE - HALF :], "scol", shifted_to("scol", 1))
    right_rim = lax.ppermute(tall[:, :, :HALF], "scol", shifted_to("scol", -1))

    near = jnp.concatenate([left_rim, tall[:, :, :HALF]], axis=2)
    blank = jnp.zeros((2, EXT, 2 * W - EXT), f32)
    far = jnp.concatenate([tall[:, :, HALF:], right_rim, blank], axis=2)
    ext = jnp.concatenate([near, far], axis=0)

    big = [pltpu.VMEM((6 * W, 2 * W), bf16), pltpu.VMEM((2 * W, 6 * W), bf16)]
    far = pl.pallas_call(
        forward_kernel,
        out_shape=jax.ShapeDtypeStruct((POSITIONS, 2 * W, 2 * W), f32),
        in_specs=[SMEM, VMEM, VMEM, VMEM],
        out_specs=HBM,
        scratch_shapes=big
        + [
            pltpu.VMEM((POSITIONS, 2 * W, 2 * W), f32),
            pltpu.SemaphoreType.DMA((POSITIONS // GROUP,)),
        ],
        compiler_params=params(58),
        cost_estimate=pl.CostEstimate(flops=0, bytes_accessed=0, transcendentals=0),
        name="forward",
    )(scalars, ext, probe_flat, tables)

    ext_grad, probe_grad = pl.pallas_call(
        lambda *refs: backward_kernel(row_dev, col_dev, *refs),
        out_shape=(
            jax.ShapeDtypeStruct((4, EXT, W), f32),
            jax.ShapeDtypeStruct((2 * MODES, W, W), f32),
        ),
        in_specs=[SMEM, VMEM, VMEM, HBM, VMEM, VMEM, VMEM, VMEM],
        out_specs=(VMEM, VMEM),
        scratch_shapes=[
            pltpu.VMEM((POSITIONS, 8, W), f32),
            pltpu.VMEM((POSITIONS, 8, W), f32),
            pltpu.VMEM((POSITIONS, W), f32),
        ]
        + big
        + [
            pltpu.VMEM((POSITIONS, W, W), f32),
            pltpu.VMEM((POSITIONS, 2 * W, 2 * W), f32),
            pltpu.SemaphoreType.DMA((POSITIONS // GROUP,)),
        ],
        compiler_params=params(50),
        cost_estimate=pl.CostEstimate(flops=8 << 30, bytes_accessed=9 << 20, transcendentals=0),
        name="backward",
    )(scalars, sums, patterns, far, ext, probe_flat, shifts, tables)

    from_below = lax.ppermute(ext_grad[:, :HALF, :], "srow", shifted_to("srow", -1))
    from_above = lax.ppermute(ext_grad[:, HALF + TILE :, :], "srow", shifted_to("srow", 1))

    near, across = two_levels(row_dev, col_dev)
    count = len(near[0])
    chunk = 2 * MODES * W // count
    part = jnp.sum(spread(probe_grad.reshape(count, chunk, W), near), axis=0)
    from_below, from_above, _ = lax.optimization_barrier((from_below, from_above, part))

    grad = ext_grad[:, HALF : HALF + TILE, :]
    grad = grad + jnp.pad(from_below, ((0, 0), (TILE - HALF, 0), (0, 0)))
    grad = grad + jnp.pad(from_above, ((0, 0), (0, TILE - HALF), (0, 0)))
    from_right = lax.ppermute(grad[:2, :, :HALF], "scol", shifted_to("scol", -1))
    from_left = lax.ppermute(
        grad[2:, :, TILE - HALF : TILE], "scol", shifted_to("scol", 1)
    )

    part = jnp.sum(spread(jnp.broadcast_to(part[None], (len(across[0]), chunk, W)), across), axis=0)
    from_right, from_left, _ = lax.optimization_barrier((from_right, from_left, part))
    total = spread(jnp.broadcast_to(part[None], (count, chunk, W)), near)

    grad = jnp.concatenate([grad[:2, :, HALF:], grad[2:, :, : TILE - HALF]], axis=2)
    grad = grad + jnp.pad(from_right, ((0, 0), (0, 0), (TILE - HALF, 0)))
    grad = grad + jnp.pad(from_left, ((0, 0), (0, 0), (0, TILE - HALF)))
    new_object = object_field - grad

    positions_all = POSITIONS * row_dev * col_dev
    new_probe = probe - (probe_rate / positions_all) * total.reshape(probe.shape)
    return new_object, new_probe


def solution(mesh):
    placed = (P("srow", "scol", None, None), P("srow", "scol", None), P(None, "srow", "scol"), P())
    return jax.shard_map(
        on_device,
        mesh=mesh,
        in_specs=placed,
        out_specs=(P(None, "srow", "scol"), P()),
        check_vma=False,
    )
```

```python
import math

import jax
import jax.numpy as jnp
import ml_dtypes
import numpy as np
from jax import lax
from jax.experimental import pallas as pl
from jax.experimental.pallas import tpu as pltpu
from jax.sharding import PartitionSpec as P

W = 128
HALF = W // 2
MODES = 2
PR = 4
PC = 4
POSITIONS = PR * PC
TILE = 72
EXT = TILE + W
GROUP = 8
AHEAD = 8

obj_rate = 0.2
probe_rate = 0.5
amp_floor = 0.1
highest = lax.Precision.HIGHEST
f32 = jnp.float32
bf16 = jnp.bfloat16


def dft_tables():
    counter = np.arange(W)
    angles = 2.0 * np.pi / W * (counter[:, None] * counter[None, :] % W)
    parts = []
    for table in (np.cos(angles), np.sin(angles)):
        high = table.astype(ml_dtypes.bfloat16)
        parts += [high, (table - high.astype(np.float64)).astype(ml_dtypes.bfloat16)]
    return np.stack(parts)


def shift_tables():
    counter = np.arange(W)
    freq = np.where(counter <= HALF, counter, counter - HALF)
    angles = 2.0 * np.pi / W * (freq[:, None] * counter[None, :] % W)
    weight = np.where((counter == 0) | (counter == HALF), 1.0, 2.0)[:, None] / W
    is_cos = (counter <= HALF)[:, None]
    cols = np.where(is_cos, np.cos(angles), np.sin(angles)) * weight
    rows = np.where(is_cos, np.cos(angles), -np.sin(angles)) * weight
    return np.stack([cols, rows]).astype(np.float32)


def split(values):
    high = values.astype(bf16)
    low = (values - high.astype(f32)).astype(bf16)
    return high, low


def fill_tables(tables_ref, right_ref, left_ref, inverse):
    for part in range(3):
        cos = tables_ref[part // 2]
        sin = tables_ref[2 + part // 2]
        plus, minus = (sin, -sin) if inverse else (-sin, sin)
        base = part * 2 * W
        right_ref[base : base + W, 0:W] = cos
        right_ref[base : base + W, W:] = plus
        right_ref[base + W : base + 2 * W, 0:W] = minus
        right_ref[base + W : base + 2 * W, W:] = cos
        scale = jnp.asarray(1.0 / W, bf16)
        left_ref[0:W, base : base + W] = cos * scale
        left_ref[0:W, base + W : base + 2 * W] = minus * scale
        left_ref[W:, base : base + W] = plus * scale
        left_ref[W:, base + W : base + 2 * W] = cos * scale


def by_parts(left, right):
    high, low = split(left)
    other_high, other_low = split(right)
    return jnp.dot(
        jnp.concatenate([high, low, high], axis=1),
        jnp.concatenate([other_high, other_high, other_low], axis=0),
        preferred_element_type=f32,
    )


def right_by(values, table):
    high, low = split(values)
    return jnp.dot(jnp.concatenate([high, low, high], axis=1), table, preferred_element_type=f32)


def left_by(table, values):
    high, low = split(values)
    return jnp.dot(table, jnp.concatenate([high, low, high], axis=0), preferred_element_type=f32)


def swap_blocks(values):
    top = jnp.concatenate([values[:W, :W], values[W:, :W]], axis=1)
    bottom = jnp.concatenate([values[:W, W:], values[W:, W:]], axis=1)
    return jnp.concatenate([top, bottom], axis=0)


def lane_iota(shape):
    return lax.broadcasted_iota(jnp.int32, shape, len(shape) - 1)


def row_iota(shape):
    return lax.broadcasted_iota(jnp.int32, shape, len(shape) - 2)


def place_of(scalars_ref, row_dev, col_dev, shape):
    position = row_iota(shape)
    row = (scalars_ref[2 * POSITIONS] * PR + position // PC).astype(f32)
    col = (scalars_ref[2 * POSITIONS + 1] * PC + position % PC).astype(f32)
    return (row + 0.5) / (PR * row_dev) - 0.5, (col + 0.5) / (PC * col_dev) - 0.5


def sums_kernel(row_dev, col_dev, scalars_ref, patterns_ref, tile_ref, out_ref, tile_out, total_ref, tilt_ref):
    tile_out[...] = tile_ref[...]
    k = row_iota((W, W))
    freq = (((k + HALF) % W) - HALF).astype(f32)
    for p in range(POSITIONS):
        pattern = patterns_ref[p]
        total_ref[p : p + 1, :] = jnp.sum(pattern, axis=0, keepdims=True)
        tilt_ref[p : p + 1, :] = jnp.sum(pattern * freq, axis=0, keepdims=True)
    lane = lane_iota((POSITIONS, W))
    col_freq = (((lane + HALF) % W) - HALF).astype(f32)
    total = total_ref[...]
    weight = jnp.sum(total, axis=1, keepdims=True)
    tilt_row = jnp.sum(tilt_ref[...], axis=1, keepdims=True)
    tilt_col = jnp.sum(total * col_freq, axis=1, keepdims=True)
    row, col = place_of(scalars_ref, row_dev, col_dev, (POSITIONS, W))
    terms = [
        weight,
        weight * row,
        weight * col,
        weight * row * row,
        weight * row * col,
        weight * col * col,
        tilt_row,
        tilt_row * row,
        tilt_row * col,
        tilt_col,
        tilt_col * row,
        tilt_col * col,
    ]
    packed = jnp.zeros((POSITIONS, W), f32)
    for i, term in enumerate(terms):
        packed = jnp.where(lane == i, term, packed)
    summed = jnp.sum(packed, axis=0, keepdims=True)
    out_ref[...] = jnp.broadcast_to(summed, out_ref.shape)


def cut_window(ext_ref, part, row, col):
    lane = lane_iota((W, W))
    shift = lax.rem(W - col, W)
    near = pltpu.roll(ext_ref[part, pl.ds(row, W), :], shift, 1)
    far = pltpu.roll(ext_ref[2 + part, pl.ds(row, W), :], shift, 1)
    return jnp.where(lane < W - col, near, far)


def forward_kernel(
    scalars_ref, ext_ref, probe_ref, tables_ref, far_out,
    right_ref, left_ref, far_ref, far_sem,
):
    fill_tables(tables_ref, right_ref, left_ref, False)

    def some(group, carried):
        places = [group * GROUP + i for i in range(GROUP)]
        waves = []
        for p in places:
            row, col = scalars_ref[2 * p], scalars_ref[2 * p + 1]
            win_re = cut_window(ext_ref, 0, row, col)
            win_im = cut_window(ext_ref, 1, row, col)
            for m in range(MODES):
                probe_re, probe_im = probe_ref[2 * m], probe_ref[2 * m + 1]
                wave_re = probe_re * win_re - probe_im * win_im
                wave_im = probe_re * win_im + probe_im * win_re
                waves.append(jnp.concatenate([wave_re, wave_im], axis=1))
        half_done = right_by(jnp.concatenate(waves, axis=0), right_ref[...])
        for i, p in enumerate(places):
            mine = half_done[i * 2 * W : (i + 1) * 2 * W]
            far_ref[p] = left_by(left_ref[...], swap_blocks(mine))
        copy_of(group).start()
        return carried

    def copy_of(group):
        part = pl.ds(group * GROUP, GROUP)
        return pltpu.make_async_copy(far_ref.at[part], far_out.at[part], far_sem.at[group])

    lax.fori_loop(0, POSITIONS // GROUP, some, 0)
    for group in range(POSITIONS // GROUP):
        copy_of(group).wait()


def descan_of(sums, row, col):
    lane = lane_iota(sums.shape)
    pick = [
        jnp.sum(jnp.where(lane == i, sums, 0.0), axis=1, keepdims=True) for i in range(12)
    ]
    weight = pick[0]
    mean_row, mean_col = pick[1] / weight, pick[2] / weight
    var_row = pick[3] - mean_row * pick[1]
    var_both = pick[4] - mean_row * pick[2]
    var_col = pick[5] - mean_col * pick[2]
    determ = var_row * var_col - var_both * var_both
    shifts = []
    for first in (6, 9):
        tilt, tilt_row, tilt_col = pick[first : first + 3]
        cov_row = tilt_row - mean_row * tilt
        cov_col = tilt_col - mean_col * tilt
        slope_row = (var_col * cov_row - var_both * cov_col) / determ
        slope_col = (var_row * cov_col - var_both * cov_row) / determ
        shifts.append(tilt / weight + slope_row * (row - mean_row) + slope_col * (col - mean_col))
    return shifts


def seed_of(line):
    return pltpu.roll(jnp.broadcast_to(line, (8, W)), 0, 1, stride=1, stride_axis=0)


def circulant(seed):
    return jnp.concatenate(
        [seed if i == 0 else pltpu.roll(seed, 8 * i, 1) for i in range(W // 8)], axis=0
    )


def backward_kernel(
    row_dev, col_dev, scalars_ref, sums_ref, patterns_ref, far_in, ext_ref, probe_ref,
    shift_ref, tables_ref, object_grad_ref, probe_grad_ref,
    cols_ref, rows_ref, nyquist_ref, right_ref, left_ref, target_ref, far_ref, far_sem,
):
    far_copies = [
        pltpu.make_async_copy(far_in.at[part], far_ref.at[part], far_sem.at[i])
        for i, part in enumerate(pl.ds(i * GROUP, GROUP) for i in range(POSITIONS // GROUP))
    ]
    for copy in far_copies:
        copy.start()

    sums = jnp.sum(sums_ref[...], axis=0, keepdims=True)
    row, col = place_of(scalars_ref, row_dev, col_dev, (POSITIONS, W))
    shift_row, shift_col = descan_of(sums, row, col)
    lane = lane_iota((POSITIONS, W))
    freq = jnp.where(lane <= HALF, lane, lane - HALF).astype(f32)
    quarter = jnp.where(lane <= HALF, 0.0, 0.25)

    def wave(shift):
        turns = freq * shift * (1.0 / W) + quarter
        return jnp.cos(2.0 * math.pi * (turns - jnp.round(turns)))

    def half_sine(shift):
        turns = shift * 0.5
        return jnp.sin(2.0 * math.pi * (turns - jnp.round(turns)))

    cols = jnp.dot(wave(shift_col), shift_ref[0], precision=highest)
    rows = jnp.dot(wave(shift_row), shift_ref[1], precision=highest)
    for p in range(POSITIONS):
        cols_ref[p] = seed_of(cols[p : p + 1])
        rows_ref[p] = seed_of(rows[p : p + 1])
    nyquist_ref[...] = half_sine(shift_row) * half_sine(shift_col) * (1.0 / (W * W))
    fill_tables(tables_ref, right_ref, left_ref, True)
    object_grad_ref[...] = jnp.zeros(object_grad_ref.shape, f32)
    probe_grad_ref[...] = jnp.zeros(probe_grad_ref.shape, f32)

    def make_targets(group, carried):
        place = row_iota((W, W)) + lane_iota((W, W))
        sign = (1 - 2 * (place & 1)).astype(f32)
        for p in [group * AHEAD + i for i in range(AHEAD)]:
            pattern = patterns_ref[p]
            moved = by_parts(pattern, circulant(cols_ref[p]))
            moved = by_parts(circulant(rows_ref[p]), moved)
            alternate = jnp.sum(pattern * sign, axis=0, keepdims=True)
            alternate = jnp.sum(alternate, axis=1, keepdims=True)
            moved = moved - sign * (alternate * nyquist_ref[pl.ds(p, 1), :])
            target_ref[p] = jnp.sqrt(jnp.maximum(moved, 0.0))
        return carried

    lax.fori_loop(0, POSITIONS // AHEAD, make_targets, 0)

    def some(group, carried):
        places = [group * GROUP + i for i in range(GROUP)]
        halves = []
        for p in places:
            far = far_ref[p]
            power = far[:W, :W] ** 2 + far[:W, W:] ** 2 + far[W:, :W] ** 2 + far[W:, W:] ** 2
            factor = 1.0 - target_ref[p] / jnp.maximum(jnp.sqrt(power), amp_floor)
            wide = jnp.concatenate([factor, factor], axis=1)
            scaled = far * jnp.concatenate([wide, wide], axis=0)
            halves.append(swap_blocks(left_by(left_ref[...], scaled)))
        back = right_by(jnp.concatenate(halves, axis=0), right_ref[...])
        lanes = lane_iota((W, W))
        windows = []
        for p in places:
            at = scalars_ref[2 * p], scalars_ref[2 * p + 1]
            windows.append((cut_window(ext_ref, 0, *at), cut_window(ext_ref, 1, *at)))
        for m in range(MODES):
            sum_re = jnp.zeros((W, W), f32)
            sum_im = jnp.zeros((W, W), f32)
            for i, p in enumerate(places):
                base = i * 2 * W + m * W
                back_re, back_im = back[base : base + W, :W], back[base : base + W, W:]
                win_re, win_im = windows[i]
                sum_re += win_re * back_re + win_im * back_im
                sum_im += win_re * back_im - win_im * back_re
            probe_grad_ref[2 * m] += sum_re
            probe_grad_ref[2 * m + 1] += sum_im
        for i, p in enumerate(places):
            grads = [jnp.zeros((W, W), f32)] * 2
            for m in range(MODES):
                base = i * 2 * W + m * W
                back_re, back_im = back[base : base + W, :W], back[base : base + W, W:]
                probe_re, probe_im = probe_ref[2 * m], probe_ref[2 * m + 1]
                grads[0] += probe_re * back_re + probe_im * back_im
                grads[1] += probe_re * back_im - probe_im * back_re
            top, left = scalars_ref[2 * p], scalars_ref[2 * p + 1]
            for part, grad in enumerate(grads):
                turned = pltpu.roll(grad, left, 1)
                inside = jnp.where(lanes >= left, turned, 0.0)
                object_grad_ref[part, pl.ds(top, W), :] += inside
                object_grad_ref[2 + part, pl.ds(top, W), :] += turned - inside
        return carried

    for copy in far_copies:
        copy.wait()
    lax.fori_loop(0, POSITIONS // GROUP, some, 0)
    probe_power = (
        probe_ref[0] ** 2 + probe_ref[1] ** 2 + probe_ref[2] ** 2 + probe_ref[3] ** 2
    )
    peak = jnp.max(jnp.max(probe_power, axis=0, keepdims=True), axis=1, keepdims=True)
    object_grad_ref[...] = object_grad_ref[...] * (obj_rate / peak)[None]


def shifted_to(axis, step):
    count = lax.axis_size(axis)
    return [(i, (i + step) % count) for i in range(count)]


def spread(values, groups=None):
    return lax.all_to_all(
        values, ("srow", "scol"), 0, 0, axis_index_groups=groups, tiled=True
    )


def two_levels(row_dev, col_dev):
    near, across = [], []
    for pair in range(col_dev // 2):
        near.append([r * col_dev + 2 * pair + c for r in range(row_dev) for c in range(2)])
    for r in range(row_dev):
        for c in range(2):
            across.append([r * col_dev + 2 * pair + c for pair in range(col_dev // 2)])
    return near, across


SMEM = pl.BlockSpec(memory_space=pltpu.SMEM)
VMEM = pl.BlockSpec(memory_space=pltpu.VMEM)
HBM = pl.BlockSpec(memory_space=pltpu.HBM)


def params(mib):
    return pltpu.CompilerParams(vmem_limit_bytes=mib * 1024 * 1024)


def on_device(patterns, offsets, object_field, probe):
    row_dev = lax.axis_size("srow")
    col_dev = lax.axis_size("scol")
    place = jnp.stack([lax.axis_index("srow"), lax.axis_index("scol")]).astype(jnp.int32)
    scalars = jnp.concatenate([offsets.reshape(2 * POSITIONS), place])
    patterns = patterns.reshape(POSITIONS, W, W)
    probe_flat = probe.reshape(2 * MODES, W, W)
    tables = jnp.asarray(dft_tables())
    shifts = jnp.asarray(shift_tables())

    above = lax.ppermute(object_field, "srow", shifted_to("srow", 1))
    below = lax.ppermute(object_field, "srow", shifted_to("srow", -1))

    sums, tile = pl.pallas_call(
        lambda *refs: sums_kernel(row_dev, col_dev, *refs),
        out_shape=(
            jax.ShapeDtypeStruct((row_dev * col_dev, W), f32),
            jax.ShapeDtypeStruct(object_field.shape, f32),
        ),
        in_specs=[SMEM, VMEM, VMEM],
        out_specs=(VMEM, VMEM),
        scratch_shapes=[pltpu.VMEM((POSITIONS, W), f32), pltpu.VMEM((POSITIONS, W), f32)],
        compiler_params=params(8),
        name="sums",
    )(scalars, patterns, object_field)
    above, below, _ = lax.optimization_barrier((above, below, sums))
    sums = spread(sums.reshape(row_dev * col_dev, 1, W)).reshape(row_dev * col_dev, W)

    tall = jnp.concatenate(
        [above[:, TILE - HALF :, :], tile, below[:, :HALF, :]], axis=1
    )
    left_rim = lax.ppermute(tall[:, :, TILE - HALF :], "scol", shifted_to("scol", 1))
    right_rim = lax.ppermute(tall[:, :, :HALF], "scol", shifted_to("scol", -1))

    near = jnp.concatenate([left_rim, tall[:, :, :HALF]], axis=2)
    blank = jnp.zeros((2, EXT, 2 * W - EXT), f32)
    far = jnp.concatenate([tall[:, :, HALF:], right_rim, blank], axis=2)
    ext = jnp.concatenate([near, far], axis=0)

    big = [pltpu.VMEM((6 * W, 2 * W), bf16), pltpu.VMEM((2 * W, 6 * W), bf16)]
    far = pl.pallas_call(
        forward_kernel,
        out_shape=jax.ShapeDtypeStruct((POSITIONS, 2 * W, 2 * W), f32),
        in_specs=[SMEM, VMEM, VMEM, VMEM],
        out_specs=HBM,
        scratch_shapes=big
        + [
            pltpu.VMEM((POSITIONS, 2 * W, 2 * W), f32),
            pltpu.SemaphoreType.DMA((POSITIONS // GROUP,)),
        ],
        compiler_params=params(58),
        cost_estimate=pl.CostEstimate(flops=0, bytes_accessed=0, transcendentals=0),
        name="forward",
    )(scalars, ext, probe_flat, tables)

    again, sums = lax.optimization_barrier((offsets, sums))
    scalars = jnp.concatenate([again.reshape(2 * POSITIONS), place])

    ext_grad, probe_grad = pl.pallas_call(
        lambda *refs: backward_kernel(row_dev, col_dev, *refs),
        out_shape=(
            jax.ShapeDtypeStruct((4, EXT, W), f32),
            jax.ShapeDtypeStruct((2 * MODES, W, W), f32),
        ),
        in_specs=[SMEM, VMEM, VMEM, HBM, VMEM, VMEM, VMEM, VMEM],
        out_specs=(VMEM, VMEM),
        scratch_shapes=[
            pltpu.VMEM((POSITIONS, 8, W), f32),
            pltpu.VMEM((POSITIONS, 8, W), f32),
            pltpu.VMEM((POSITIONS, W), f32),
        ]
        + big
        + [
            pltpu.VMEM((POSITIONS, W, W), f32),
            pltpu.VMEM((POSITIONS, 2 * W, 2 * W), f32),
            pltpu.SemaphoreType.DMA((POSITIONS // GROUP,)),
        ],
        compiler_params=params(50),
        cost_estimate=pl.CostEstimate(flops=8 << 30, bytes_accessed=9 << 20, transcendentals=0),
        name="backward",
    )(scalars, sums, patterns, far, ext, probe_flat, shifts, tables)

    from_below = lax.ppermute(ext_grad[:, :HALF, :], "srow", shifted_to("srow", -1))
    from_above = lax.ppermute(ext_grad[:, HALF + TILE :, :], "srow", shifted_to("srow", 1))

    near, across = two_levels(row_dev, col_dev)
    count = len(near[0])
    chunk = 2 * MODES * W // count
    part = jnp.sum(spread(probe_grad.reshape(count, chunk, W), near), axis=0)
    from_below, from_above, _ = lax.optimization_barrier((from_below, from_above, part))

    grad = ext_grad[:, HALF : HALF + TILE, :]
    grad = grad + jnp.pad(from_below, ((0, 0), (TILE - HALF, 0), (0, 0)))
    grad = grad + jnp.pad(from_above, ((0, 0), (0, TILE - HALF), (0, 0)))
    from_right = lax.ppermute(grad[:2, :, :HALF], "scol", shifted_to("scol", -1))
    from_left = lax.ppermute(
        grad[2:, :, TILE - HALF : TILE], "scol", shifted_to("scol", 1)
    )

    part = jnp.sum(spread(jnp.broadcast_to(part[None], (len(across[0]), chunk, W)), across), axis=0)
    from_right, from_left, _ = lax.optimization_barrier((from_right, from_left, part))
    total = spread(jnp.broadcast_to(part[None], (count, chunk, W)), near)

    grad = jnp.concatenate([grad[:2, :, HALF:], grad[2:, :, : TILE - HALF]], axis=2)
    grad = grad + jnp.pad(from_right, ((0, 0), (0, 0), (TILE - HALF, 0)))
    grad = grad + jnp.pad(from_left, ((0, 0), (0, 0), (0, TILE - HALF)))
    new_object = object_field - grad

    positions_all = POSITIONS * row_dev * col_dev
    new_probe = probe - (probe_rate / positions_all) * total.reshape(probe.shape)
    return new_object, new_probe


def solution(mesh):
    placed = (P("srow", "scol", None, None), P("srow", "scol", None), P(None, "srow", "scol"), P())
    return jax.shard_map(
        on_device,
        mesh=mesh,
        in_specs=placed,
        out_specs=(P(None, "srow", "scol"), P()),
        check_vma=False,
    )
```

```python
import math

import jax
import jax.numpy as jnp
import ml_dtypes
import numpy as np
from jax import lax
from jax.experimental import pallas as pl
from jax.experimental.pallas import tpu as pltpu
from jax.sharding import PartitionSpec as P

W = 128
HALF = W // 2
MODES = 2
PR = 4
PC = 4
POSITIONS = PR * PC
TILE = 72
EXT = TILE + W
GROUP = 16
AHEAD = 8

obj_rate = 0.2
probe_rate = 0.5
amp_floor = 0.1
highest = lax.Precision.HIGHEST
f32 = jnp.float32
bf16 = jnp.bfloat16


def dft_tables():
    counter = np.arange(W)
    angles = 2.0 * np.pi / W * (counter[:, None] * counter[None, :] % W)
    parts = []
    for table in (np.cos(angles), np.sin(angles)):
        high = table.astype(ml_dtypes.bfloat16)
        parts += [high, (table - high.astype(np.float64)).astype(ml_dtypes.bfloat16)]
    return np.stack(parts)


def shift_tables():
    counter = np.arange(W)
    freq = np.where(counter <= HALF, counter, counter - HALF)
    angles = 2.0 * np.pi / W * (freq[:, None] * counter[None, :] % W)
    weight = np.where((counter == 0) | (counter == HALF), 1.0, 2.0)[:, None] / W
    is_cos = (counter <= HALF)[:, None]
    cols = np.where(is_cos, np.cos(angles), np.sin(angles)) * weight
    rows = np.where(is_cos, np.cos(angles), -np.sin(angles)) * weight
    return np.stack([cols, rows]).astype(np.float32)


def split(values):
    high = values.astype(bf16)
    low = (values - high.astype(f32)).astype(bf16)
    return high, low


def fill_tables(tables_ref, right_ref, left_ref, inverse):
    for part in range(3):
        cos = tables_ref[part // 2]
        sin = tables_ref[2 + part // 2]
        plus, minus = (sin, -sin) if inverse else (-sin, sin)
        base = part * 2 * W
        right_ref[base : base + W, 0:W] = cos
        right_ref[base : base + W, W:] = plus
        right_ref[base + W : base + 2 * W, 0:W] = minus
        right_ref[base + W : base + 2 * W, W:] = cos
        scale = jnp.asarray(1.0 / W, bf16)
        left_ref[0:W, base : base + W] = cos * scale
        left_ref[0:W, base + W : base + 2 * W] = minus * scale
        left_ref[W:, base : base + W] = plus * scale
        left_ref[W:, base + W : base + 2 * W] = cos * scale


def by_parts(left, right):
    high, low = split(left)
    other_high, other_low = split(right)
    return jnp.dot(
        jnp.concatenate([high, low, high], axis=1),
        jnp.concatenate([other_high, other_high, other_low], axis=0),
        preferred_element_type=f32,
    )


def right_by(values, table):
    high, low = split(values)
    return jnp.dot(jnp.concatenate([high, low, high], axis=1), table, preferred_element_type=f32)


def left_by(table, values):
    high, low = split(values)
    return jnp.dot(table, jnp.concatenate([high, low, high], axis=0), preferred_element_type=f32)


def swap_blocks(values):
    top = jnp.concatenate([values[:W, :W], values[W:, :W]], axis=1)
    bottom = jnp.concatenate([values[:W, W:], values[W:, W:]], axis=1)
    return jnp.concatenate([top, bottom], axis=0)


def lane_iota(shape):
    return lax.broadcasted_iota(jnp.int32, shape, len(shape) - 1)


def row_iota(shape):
    return lax.broadcasted_iota(jnp.int32, shape, len(shape) - 2)


def place_of(scalars_ref, row_dev, col_dev, shape):
    position = row_iota(shape)
    row = (scalars_ref[2 * POSITIONS] * PR + position // PC).astype(f32)
    col = (scalars_ref[2 * POSITIONS + 1] * PC + position % PC).astype(f32)
    return (row + 0.5) / (PR * row_dev) - 0.5, (col + 0.5) / (PC * col_dev) - 0.5


def sums_kernel(row_dev, col_dev, scalars_ref, patterns_ref, tile_ref, out_ref, tile_out, total_ref, tilt_ref):
    tile_out[...] = tile_ref[...]
    k = row_iota((W, W))
    freq = (((k + HALF) % W) - HALF).astype(f32)
    for p in range(POSITIONS):
        pattern = patterns_ref[p]
        total_ref[p : p + 1, :] = jnp.sum(pattern, axis=0, keepdims=True)
        tilt_ref[p : p + 1, :] = jnp.sum(pattern * freq, axis=0, keepdims=True)
    lane = lane_iota((POSITIONS, W))
    col_freq = (((lane + HALF) % W) - HALF).astype(f32)
    total = total_ref[...]
    weight = jnp.sum(total, axis=1, keepdims=True)
    tilt_row = jnp.sum(tilt_ref[...], axis=1, keepdims=True)
    tilt_col = jnp.sum(total * col_freq, axis=1, keepdims=True)
    row, col = place_of(scalars_ref, row_dev, col_dev, (POSITIONS, W))
    terms = [
        weight,
        weight * row,
        weight * col,
        weight * row * row,
        weight * row * col,
        weight * col * col,
        tilt_row,
        tilt_row * row,
        tilt_row * col,
        tilt_col,
        tilt_col * row,
        tilt_col * col,
    ]
    packed = jnp.zeros((POSITIONS, W), f32)
    for i, term in enumerate(terms):
        packed = jnp.where(lane == i, term, packed)
    summed = jnp.sum(packed, axis=0, keepdims=True)
    out_ref[...] = jnp.broadcast_to(summed, out_ref.shape)


def cut_window(ext_ref, part, row, col):
    lane = lane_iota((W, W))
    shift = lax.rem(W - col, W)
    near = pltpu.roll(ext_ref[part, pl.ds(row, W), :], shift, 1)
    far = pltpu.roll(ext_ref[2 + part, pl.ds(row, W), :], shift, 1)
    return jnp.where(lane < W - col, near, far)


def forward_kernel(
    scalars_ref, ext_ref, probe_ref, tables_ref, far_out,
    right_ref, left_ref, far_ref, far_sem,
):
    fill_tables(tables_ref, right_ref, left_ref, False)

    def some(group, carried):
        places = [group * GROUP + i for i in range(GROUP)]
        waves = []
        for p in places:
            row, col = scalars_ref[2 * p], scalars_ref[2 * p + 1]
            win_re = cut_window(ext_ref, 0, row, col)
            win_im = cut_window(ext_ref, 1, row, col)
            for m in range(MODES):
                probe_re, probe_im = probe_ref[2 * m], probe_ref[2 * m + 1]
                wave_re = probe_re * win_re - probe_im * win_im
                wave_im = probe_re * win_im + probe_im * win_re
                waves.append(jnp.concatenate([wave_re, wave_im], axis=1))
        half_done = right_by(jnp.concatenate(waves, axis=0), right_ref[...])
        for i, p in enumerate(places):
            mine = half_done[i * 2 * W : (i + 1) * 2 * W]
            far_ref[p] = left_by(left_ref[...], swap_blocks(mine))
        copy_of(group).start()
        return carried

    def copy_of(group):
        part = pl.ds(group * GROUP, GROUP)
        return pltpu.make_async_copy(far_ref.at[part], far_out.at[part], far_sem.at[group])

    lax.fori_loop(0, POSITIONS // GROUP, some, 0)
    for group in range(POSITIONS // GROUP):
        copy_of(group).wait()


def descan_of(sums, row, col):
    lane = lane_iota(sums.shape)
    pick = [
        jnp.sum(jnp.where(lane == i, sums, 0.0), axis=1, keepdims=True) for i in range(12)
    ]
    weight = pick[0]
    mean_row, mean_col = pick[1] / weight, pick[2] / weight
    var_row = pick[3] - mean_row * pick[1]
    var_both = pick[4] - mean_row * pick[2]
    var_col = pick[5] - mean_col * pick[2]
    determ = var_row * var_col - var_both * var_both
    shifts = []
    for first in (6, 9):
        tilt, tilt_row, tilt_col = pick[first : first + 3]
        cov_row = tilt_row - mean_row * tilt
        cov_col = tilt_col - mean_col * tilt
        slope_row = (var_col * cov_row - var_both * cov_col) / determ
        slope_col = (var_row * cov_col - var_both * cov_row) / determ
        shifts.append(tilt / weight + slope_row * (row - mean_row) + slope_col * (col - mean_col))
    return shifts


def seed_of(line):
    return pltpu.roll(jnp.broadcast_to(line, (8, W)), 0, 1, stride=1, stride_axis=0)


def circulant(seed):
    return jnp.concatenate(
        [seed if i == 0 else pltpu.roll(seed, 8 * i, 1) for i in range(W // 8)], axis=0
    )


def backward_kernel(
    row_dev, col_dev, scalars_ref, sums_ref, patterns_ref, far_in, ext_ref, probe_ref,
    shift_ref, tables_ref, object_grad_ref, probe_grad_ref,
    cols_ref, rows_ref, nyquist_ref, right_ref, left_ref, target_ref, far_ref, far_sem,
):
    far_copies = [
        pltpu.make_async_copy(far_in.at[part], far_ref.at[part], far_sem.at[i])
        for i, part in enumerate(pl.ds(i * GROUP, GROUP) for i in range(POSITIONS // GROUP))
    ]
    for copy in far_copies:
        copy.start()

    sums = jnp.sum(sums_ref[...], axis=0, keepdims=True)
    row, col = place_of(scalars_ref, row_dev, col_dev, (POSITIONS, W))
    shift_row, shift_col = descan_of(sums, row, col)
    lane = lane_iota((POSITIONS, W))
    freq = jnp.where(lane <= HALF, lane, lane - HALF).astype(f32)
    quarter = jnp.where(lane <= HALF, 0.0, 0.25)

    def wave(shift):
        turns = freq * shift * (1.0 / W) + quarter
        return jnp.cos(2.0 * math.pi * (turns - jnp.round(turns)))

    def half_sine(shift):
        turns = shift * 0.5
        return jnp.sin(2.0 * math.pi * (turns - jnp.round(turns)))

    cols = jnp.dot(wave(shift_col), shift_ref[0], precision=highest)
    rows = jnp.dot(wave(shift_row), shift_ref[1], precision=highest)
    for p in range(POSITIONS):
        cols_ref[p] = seed_of(cols[p : p + 1])
        rows_ref[p] = seed_of(rows[p : p + 1])
    nyquist_ref[...] = half_sine(shift_row) * half_sine(shift_col) * (1.0 / (W * W))
    fill_tables(tables_ref, right_ref, left_ref, True)
    object_grad_ref[...] = jnp.zeros(object_grad_ref.shape, f32)
    probe_grad_ref[...] = jnp.zeros(probe_grad_ref.shape, f32)

    def make_targets(group, carried):
        place = row_iota((W, W)) + lane_iota((W, W))
        sign = (1 - 2 * (place & 1)).astype(f32)
        for p in [group * AHEAD + i for i in range(AHEAD)]:
            pattern = patterns_ref[p]
            moved = by_parts(pattern, circulant(cols_ref[p]))
            moved = by_parts(circulant(rows_ref[p]), moved)
            alternate = jnp.sum(pattern * sign, axis=0, keepdims=True)
            alternate = jnp.sum(alternate, axis=1, keepdims=True)
            moved = moved - sign * (alternate * nyquist_ref[pl.ds(p, 1), :])
            target_ref[p] = jnp.sqrt(jnp.maximum(moved, 0.0))
        return carried

    lax.fori_loop(0, POSITIONS // AHEAD, make_targets, 0)

    def some(group, carried):
        places = [group * GROUP + i for i in range(GROUP)]
        halves = []
        for p in places:
            far = far_ref[p]
            power = far[:W, :W] ** 2 + far[:W, W:] ** 2 + far[W:, :W] ** 2 + far[W:, W:] ** 2
            factor = 1.0 - target_ref[p] / jnp.maximum(jnp.sqrt(power), amp_floor)
            wide = jnp.concatenate([factor, factor], axis=1)
            scaled = far * jnp.concatenate([wide, wide], axis=0)
            halves.append(swap_blocks(left_by(left_ref[...], scaled)))
        back = right_by(jnp.concatenate(halves, axis=0), right_ref[...])
        lanes = lane_iota((W, W))
        windows = []
        for p in places:
            at = scalars_ref[2 * p], scalars_ref[2 * p + 1]
            windows.append((cut_window(ext_ref, 0, *at), cut_window(ext_ref, 1, *at)))
        for m in range(MODES):
            sum_re = jnp.zeros((W, W), f32)
            sum_im = jnp.zeros((W, W), f32)
            for i, p in enumerate(places):
                base = i * 2 * W + m * W
                back_re, back_im = back[base : base + W, :W], back[base : base + W, W:]
                win_re, win_im = windows[i]
                sum_re += win_re * back_re + win_im * back_im
                sum_im += win_re * back_im - win_im * back_re
            probe_grad_ref[2 * m] += sum_re
            probe_grad_ref[2 * m + 1] += sum_im
        for i, p in enumerate(places):
            grads = [jnp.zeros((W, W), f32)] * 2
            for m in range(MODES):
                base = i * 2 * W + m * W
                back_re, back_im = back[base : base + W, :W], back[base : base + W, W:]
                probe_re, probe_im = probe_ref[2 * m], probe_ref[2 * m + 1]
                grads[0] += probe_re * back_re + probe_im * back_im
                grads[1] += probe_re * back_im - probe_im * back_re
            top, left = scalars_ref[2 * p], scalars_ref[2 * p + 1]
            for part, grad in enumerate(grads):
                turned = pltpu.roll(grad, left, 1)
                inside = jnp.where(lanes >= left, turned, 0.0)
                object_grad_ref[part, pl.ds(top, W), :] += inside
                object_grad_ref[2 + part, pl.ds(top, W), :] += turned - inside
        return carried

    for copy in far_copies:
        copy.wait()
    lax.fori_loop(0, POSITIONS // GROUP, some, 0)
    probe_power = (
        probe_ref[0] ** 2 + probe_ref[1] ** 2 + probe_ref[2] ** 2 + probe_ref[3] ** 2
    )
    peak = jnp.max(jnp.max(probe_power, axis=0, keepdims=True), axis=1, keepdims=True)
    object_grad_ref[...] = object_grad_ref[...] * (obj_rate / peak)[None]


def shifted_to(axis, step):
    count = lax.axis_size(axis)
    return [(i, (i + step) % count) for i in range(count)]


def spread(values, groups=None):
    return lax.all_to_all(
        values, ("srow", "scol"), 0, 0, axis_index_groups=groups, tiled=True
    )


def two_levels(row_dev, col_dev):
    near, across = [], []
    for pair in range(col_dev // 2):
        near.append([r * col_dev + 2 * pair + c for r in range(row_dev) for c in range(2)])
    for r in range(row_dev):
        for c in range(2):
            across.append([r * col_dev + 2 * pair + c for pair in range(col_dev // 2)])
    return near, across


SMEM = pl.BlockSpec(memory_space=pltpu.SMEM)
VMEM = pl.BlockSpec(memory_space=pltpu.VMEM)
HBM = pl.BlockSpec(memory_space=pltpu.HBM)


def params(mib):
    return pltpu.CompilerParams(vmem_limit_bytes=mib * 1024 * 1024)


def on_device(patterns, offsets, object_field, probe):
    row_dev = lax.axis_size("srow")
    col_dev = lax.axis_size("scol")
    place = jnp.stack([lax.axis_index("srow"), lax.axis_index("scol")]).astype(jnp.int32)
    scalars = jnp.concatenate([offsets.reshape(2 * POSITIONS), place])
    patterns = patterns.reshape(POSITIONS, W, W)
    probe_flat = probe.reshape(2 * MODES, W, W)
    tables = jnp.asarray(dft_tables())
    shifts = jnp.asarray(shift_tables())

    above = lax.ppermute(object_field, "srow", shifted_to("srow", 1))
    below = lax.ppermute(object_field, "srow", shifted_to("srow", -1))

    sums, tile = pl.pallas_call(
        lambda *refs: sums_kernel(row_dev, col_dev, *refs),
        out_shape=(
            jax.ShapeDtypeStruct((row_dev * col_dev, W), f32),
            jax.ShapeDtypeStruct(object_field.shape, f32),
        ),
        in_specs=[SMEM, VMEM, VMEM],
        out_specs=(VMEM, VMEM),
        scratch_shapes=[pltpu.VMEM((POSITIONS, W), f32), pltpu.VMEM((POSITIONS, W), f32)],
        compiler_params=params(8),
        name="sums",
    )(scalars, patterns, object_field)
    above, below, _ = lax.optimization_barrier((above, below, sums))
    sums = spread(sums.reshape(row_dev * col_dev, 1, W)).reshape(row_dev * col_dev, W)

    tall = jnp.concatenate(
        [above[:, TILE - HALF :, :], tile, below[:, :HALF, :]], axis=1
    )
    left_rim = lax.ppermute(tall[:, :, TILE - HALF :], "scol", shifted_to("scol", 1))
    right_rim = lax.ppermute(tall[:, :, :HALF], "scol", shifted_to("scol", -1))

    near = jnp.concatenate([left_rim, tall[:, :, :HALF]], axis=2)
    blank = jnp.zeros((2, EXT, 2 * W - EXT), f32)
    far = jnp.concatenate([tall[:, :, HALF:], right_rim, blank], axis=2)
    ext = jnp.concatenate([near, far], axis=0)

    big = [pltpu.VMEM((6 * W, 2 * W), bf16), pltpu.VMEM((2 * W, 6 * W), bf16)]
    far = pl.pallas_call(
        forward_kernel,
        out_shape=jax.ShapeDtypeStruct((POSITIONS, 2 * W, 2 * W), f32),
        in_specs=[SMEM, VMEM, VMEM, VMEM],
        out_specs=HBM,
        scratch_shapes=big
        + [
            pltpu.VMEM((POSITIONS, 2 * W, 2 * W), f32),
            pltpu.SemaphoreType.DMA((POSITIONS // GROUP,)),
        ],
        compiler_params=params(58),
        cost_estimate=pl.CostEstimate(flops=0, bytes_accessed=0, transcendentals=0),
        name="forward",
    )(scalars, ext, probe_flat, tables)

    again, sums = lax.optimization_barrier((offsets, sums))
    scalars = jnp.concatenate([again.reshape(2 * POSITIONS), place])

    ext_grad, probe_grad = pl.pallas_call(
        lambda *refs: backward_kernel(row_dev, col_dev, *refs),
        out_shape=(
            jax.ShapeDtypeStruct((4, EXT, W), f32),
            jax.ShapeDtypeStruct((2 * MODES, W, W), f32),
        ),
        in_specs=[SMEM, VMEM, VMEM, HBM, VMEM, VMEM, VMEM, VMEM],
        out_specs=(VMEM, VMEM),
        scratch_shapes=[
            pltpu.VMEM((POSITIONS, 8, W), f32),
            pltpu.VMEM((POSITIONS, 8, W), f32),
            pltpu.VMEM((POSITIONS, W), f32),
        ]
        + big
        + [
            pltpu.VMEM((POSITIONS, W, W), f32),
            pltpu.VMEM((POSITIONS, 2 * W, 2 * W), f32),
            pltpu.SemaphoreType.DMA((POSITIONS // GROUP,)),
        ],
        compiler_params=params(50),
        cost_estimate=pl.CostEstimate(flops=8 << 30, bytes_accessed=9 << 20, transcendentals=0),
        name="backward",
    )(scalars, sums, patterns, far, ext, probe_flat, shifts, tables)

    from_below = lax.ppermute(ext_grad[:, :HALF, :], "srow", shifted_to("srow", -1))
    from_above = lax.ppermute(ext_grad[:, HALF + TILE :, :], "srow", shifted_to("srow", 1))

    near, across = two_levels(row_dev, col_dev)
    count = len(near[0])
    chunk = 2 * MODES * W // count
    part = jnp.sum(spread(probe_grad.reshape(count, chunk, W), near), axis=0)
    from_below, from_above, _ = lax.optimization_barrier((from_below, from_above, part))

    grad = ext_grad[:, HALF : HALF + TILE, :]
    grad = grad + jnp.pad(from_below, ((0, 0), (TILE - HALF, 0), (0, 0)))
    grad = grad + jnp.pad(from_above, ((0, 0), (0, TILE - HALF), (0, 0)))
    from_right = lax.ppermute(grad[:2, :, :HALF], "scol", shifted_to("scol", -1))
    from_left = lax.ppermute(
        grad[2:, :, TILE - HALF : TILE], "scol", shifted_to("scol", 1)
    )

    part = jnp.sum(spread(jnp.broadcast_to(part[None], (len(across[0]), chunk, W)), across), axis=0)
    from_right, from_left, _ = lax.optimization_barrier((from_right, from_left, part))
    total = spread(jnp.broadcast_to(part[None], (count, chunk, W)), near)

    grad = jnp.concatenate([grad[:2, :, HALF:], grad[2:, :, : TILE - HALF]], axis=2)
    grad = grad + jnp.pad(from_right, ((0, 0), (0, 0), (TILE - HALF, 0)))
    grad = grad + jnp.pad(from_left, ((0, 0), (0, 0), (0, TILE - HALF)))
    new_object = object_field - grad

    positions_all = POSITIONS * row_dev * col_dev
    new_probe = probe - (probe_rate / positions_all) * total.reshape(probe.shape)
    return new_object, new_probe


def solution(mesh):
    placed = (P("srow", "scol", None, None), P("srow", "scol", None), P(None, "srow", "scol"), P())
    return jax.shard_map(
        on_device,
        mesh=mesh,
        in_specs=placed,
        out_specs=(P(None, "srow", "scol"), P()),
        check_vma=False,
    )
```
